256 devices in a mesh: blk: 64 (over y_hi, z, x), span: 4 (over y_lo, core).
Axes of the slice: x: 4, y: 4 (y_hi: 2, y_lo: 2; y = y_hi * 2 + y_lo), z: 8, core: 2. Of those that a mesh axis runs over, the one named last changes fastest.
Arguments:
- home_table: float32 [400, 65536], P(None, ('blk', 'span')), may hold values from -3 to 3
- home_state: float32 [65536], P(('blk', 'span')), may hold values from 0.0001 to 1
- visit_table: float32 [400, 65536], P(None, ('blk', 'span')), may hold values from -3 to 3
- visit_state: float32 [65536], P(('blk', 'span')), may hold values from 0.0001 to 1
- relation_table: float32 [400, 7424], P(None, ('blk', 'span')), may hold values from -2 to 2
- relation_state: float32 [7424], P(('blk', 'span')), may hold values from 0.0001 to 1
- edge_src: int32 [64, 4, 1024], P('blk', 'span'), may hold values from 0 to 1023
- edge_rel: int32 [64, 4, 1024], P('blk', 'span'), may hold values from 0 to 7423
- edge_dst: int32 [64, 4, 1024], P('blk', 'span'), may hold values from 0 to 255
- edge_count: int32 [64, 4], P('blk', 'span'), may hold values from 65 to 1024, as said below
- neg_rows: int32 [64, 1024], P('blk'), may hold values from 0 to 1023
Outputs:
- new_home_table: float32 [400, 65536], P(None, ('blk', 'span'))
- new_home_state: float32 [65536], P(('blk', 'span'))
- new_visit_table: float32 [400, 65536], P(None, ('blk', 'span'))
- new_visit_state: float32 [65536], P(('blk', 'span'))
- new_relation_table: float32 [400, 7424], P(None, ('blk', 'span'))
- new_relation_state: float32 [7424], P(('blk', 'span'))
The draws below stay inside these ranges and needn't reach their ends.
Inputs may be any that keep to these rules, and one draw needn't show every extreme that they name: `edge_count`: the counts of one bucket sum to at most 1536; some bucket reaches that sum and some span index reaches 1024.
All inputs are finite; a program needn't handle non-finite values.
Results may differ from the reference program's by a relative error of at most 0.0023.
Values may be sent and summed in bfloat16 or wider, within the bound.
A program may use at most 128 MiB of HBM per device.

```python
import math
import jax
import jax.numpy as jnp
from jax import lax

D = 400
REL = 7424
NEG = 1024
R_DEV = 256
CAP = 1024
RP = 1024
ROWS = 65536
N_BLK = 64
N_SPAN = 4


def draw_edge_count(key, part):
    key = jax.random.fold_in(key, 11)
    heavy_key, amount_key, light_key, special_key = jax.random.split(key, 4)
    heavy_at = jax.random.randint(heavy_key, (N_BLK,), 0, N_SPAN)
    heavy_count = jax.random.randint(amount_key, (N_BLK,), CAP // 2, CAP + 1)
    light_count = jax.random.randint(light_key, (N_BLK, N_SPAN), CAP // 16 + 1, CAP // 8 + 1)
    special = jax.random.randint(special_key, (), 0, N_BLK)
    span_pos = jnp.arange(N_SPAN, dtype=jnp.int32)
    rank_in = (span_pos[None, :] - heavy_at[:, None]) % N_SPAN
    counts = jnp.where(rank_in == 0, heavy_count[:, None], light_count)
    second_count = CAP // 4 + CAP // 8 - CAP // 16 - 1
    special_counts = jnp.where(rank_in == 0, CAP, jnp.where(rank_in == 1, second_count, jnp.where(rank_in == 2, CAP // 8, CAP // 16 + 1)))
    bucket_pos = jnp.arange(N_BLK, dtype=jnp.int32)
    counts = jnp.where(bucket_pos[:, None] == special, special_counts, counts)
    return counts.astype(jnp.int32)


def touch_ends(result, key, low, top_value):
    longest = result.shape.index(max(result.shape))
    spots = []
    for shift in (0, 1):
        where = [jax.random.randint(jax.random.fold_in(key, axis), (), 0, length) for axis, length in enumerate(result.shape)]
        where[longest] = (where[longest] + shift) % result.shape[longest]
        spots.append(tuple(where))
    return result.at[spots[0]].set(low).at[spots[1]].set(top_value)


def block_scale(rng, extent, cuts, low, top_value):
    factor_of = 1.0
    for dim, parts in cuts:
        steps = jax.random.uniform(jax.random.fold_in(jax.random.fold_in(rng, 6), dim), (parts,), jnp.float32, low / len(cuts), top_value / len(cuts))
        factor_of = factor_of * jnp.repeat(jnp.exp(steps), extent[dim] // parts).reshape((-1,) + (1,) * (len(extent) - 1 - dim))
    return factor_of


def noise(own_key, shape, spread, reach, pieces=(), kind=jnp.bfloat16):
    loudness = block_scale(own_key, shape, pieces, -0.22, 0.18) if pieces else 1.0
    values = jax.random.normal(own_key, shape, jnp.float32) * spread * loudness
    return jnp.minimum(jnp.maximum(values, -reach), reach).astype(kind)


def setup_inputs(seed: int = 0) -> dict:
    splits = jax.random.split(jax.random.key(seed), 12)
    return {
        "home_table": noise(splits[0], (D, ROWS), 0.5, 3.0, ((1, 256),), jnp.float32),
        "home_state": jnp.clip(jnp.exp(math.log(1.0) - 9.2103404 * jax.random.uniform(splits[1], (ROWS,), jnp.float32) ** block_scale(splits[1], (ROWS,), ((0, 256),), -0.2, 0.2)), 0.0001, 1.0),
        "visit_table": noise(splits[2], (D, ROWS), 0.5, 3.0, ((1, 256),), jnp.float32),
        "visit_state": jnp.clip(jnp.exp(math.log(1.0) - 9.2103404 * jax.random.uniform(splits[3], (ROWS,), jnp.float32) ** block_scale(splits[3], (ROWS,), ((0, 256),), -0.2, 0.2)), 0.0001, 1.0),
        "relation_table": noise(splits[4], (D, REL), 0.3, 2.0, ((1, 256),), jnp.float32),
        "relation_state": jnp.clip(jnp.exp(math.log(1.0) - 9.2103404 * jax.random.uniform(splits[5], (REL,), jnp.float32) ** block_scale(splits[5], (REL,), ((0, 256),), -0.2, 0.2)), 0.0001, 1.0),
        "edge_src": touch_ends(jax.random.randint(splits[6], (N_BLK, N_SPAN, CAP), 0, RP), jax.random.fold_in(splits[6], 1), 0, RP - 1).astype(jnp.int32),
        "edge_rel": touch_ends(jax.random.randint(splits[7], (N_BLK, N_SPAN, CAP), 0, REL), jax.random.fold_in(splits[7], 1), 0, REL - 1).astype(jnp.int32),
        "edge_dst": touch_ends(jax.random.randint(splits[8], (N_BLK, N_SPAN, CAP), 0, R_DEV), jax.random.fold_in(splits[8], 1), 0, R_DEV - 1).astype(jnp.int32),
        "edge_count": draw_edge_count(jax.random.fold_in(splits[11], 71), 0),
        "neg_rows": touch_ends(jax.random.randint(splits[10], (N_BLK, NEG), 0, RP), jax.random.fold_in(splits[10], 1), 0, RP - 1).astype(jnp.int32),
    }


LEARN_RATE = 0.1
ADAGRAD_EPS = 1e-10

def complex_apply(left, right):
    middle = left.shape[0] // 2
    left_re = left[:middle].astype(jnp.float32)
    left_im = left[middle:].astype(jnp.float32)
    right_re = right[:middle].astype(jnp.float32)
    right_im = right[middle:].astype(jnp.float32)
    return jnp.concatenate([left_re * right_re - left_im * right_im, left_re * right_im + left_im * right_re], axis=0)

def conj_apply(left, grad_in):
    middle = left.shape[0] // 2
    left_re = left[:middle].astype(jnp.float32)
    left_im = left[middle:].astype(jnp.float32)
    grad_re = grad_in[:middle]
    grad_im = grad_in[middle:]
    return jnp.concatenate([left_re * grad_re + left_im * grad_im, left_re * grad_im - left_im * grad_re], axis=0)

def edge_grads(source, dest, relation, live_mask, negatives):
    trans = lax.optimization_barrier(complex_apply(relation, dest).astype(jnp.bfloat16))
    trans_wide = trans.astype(jnp.float32)
    positive = lax.optimization_barrier(jnp.sum(source.astype(jnp.float32) * trans_wide, axis=0))
    neg_score = jnp.dot(trans.T, negatives, preferred_element_type=jnp.float32)
    pos_weight = -live_mask * jax.nn.sigmoid(-positive)
    neg_weight = (live_mask[:, None] * jax.nn.sigmoid(neg_score) / negatives.shape[1]).astype(jnp.bfloat16)
    neg_pull = jnp.dot(negatives, neg_weight.T, preferred_element_type=jnp.float32)
    grad_trans = pos_weight[None, :] * source.astype(jnp.float32) + neg_pull
    grad_source = pos_weight[None, :] * trans_wide
    grad_dest = conj_apply(relation, grad_trans)
    grad_relation = conj_apply(dest, grad_trans)
    grad_negative = jnp.dot(trans, neg_weight, preferred_element_type=jnp.float32)
    return (grad_source, grad_dest, grad_relation, grad_negative)

def adagrad(table, state, grad_in):
    state_new = state + lax.optimization_barrier(jnp.mean(grad_in * grad_in, axis=0))
    return (table - LEARN_RATE * grad_in / (jnp.sqrt(state_new)[None, :] + ADAGRAD_EPS), state_new)

def reference(home_table, home_state, visit_table, visit_state, relation_table, relation_state, edge_src, edge_rel, edge_dst, edge_count, neg_rows):
    features = home_table.shape[0]
    part_rows = R_DEV * N_SPAN
    relation_low = relation_table.astype(jnp.bfloat16)
    slot_pos = jnp.arange(CAP, dtype=jnp.int32)

    def bucket_step(relation_acc, bucket):
        first_col = bucket * part_rows
        home_part = lax.dynamic_slice_in_dim(home_table, first_col, part_rows, 1)
        home_stat = lax.dynamic_slice_in_dim(home_state, first_col, part_rows, 0)
        visit_part = lax.dynamic_slice_in_dim(visit_table, first_col, part_rows, 1)
        visit_stat = lax.dynamic_slice_in_dim(visit_state, first_col, part_rows, 0)
        home_low = home_part.astype(jnp.bfloat16)
        visit_low = visit_part.astype(jnp.bfloat16)
        negatives = jnp.take(home_low, neg_rows[bucket], axis=1)

        def span_step(totals, span_index):
            home_acc, visit_acc, neg_acc, rel_acc = totals
            source_rows = edge_src[bucket, span_index]
            relation_ids = edge_rel[bucket, span_index]
            dest_rows = (span_index * R_DEV + edge_dst[bucket, span_index]).astype(jnp.int32)
            live_mask = (slot_pos < edge_count[bucket, span_index]).astype(jnp.float32)
            gradients = edge_grads(jnp.take(home_low, source_rows, axis=1), jnp.take(visit_low, dest_rows, axis=1), jnp.take(relation_low, relation_ids, axis=1), live_mask, negatives)
            home_acc = home_acc.at[:, source_rows].add(gradients[0])
            visit_acc = visit_acc.at[:, dest_rows].add(gradients[1])
            rel_acc = rel_acc.at[:, relation_ids].add(gradients[2])
            return ((home_acc, visit_acc, neg_acc + gradients[3], rel_acc), None)
        zeros_table = jnp.zeros((features, part_rows), jnp.float32)
        initial = (zeros_table, zeros_table, jnp.zeros((features, NEG), jnp.float32), relation_acc)
        totals, ignored = lax.scan(span_step, initial, jnp.arange(N_SPAN, dtype=jnp.int32))
        home_acc, visit_acc, neg_acc, relation_acc = totals
        home_acc = home_acc.at[:, neg_rows[bucket]].add(neg_acc)
        new_home, new_home_stat = adagrad(home_part, home_stat, home_acc)
        new_visit, new_visit_stat = adagrad(visit_part, visit_stat, visit_acc)
        return (relation_acc, (new_home, new_home_stat, new_visit, new_visit_stat))
    relation_acc, stacked = lax.scan(bucket_step, jnp.zeros((features, REL), jnp.float32), jnp.arange(N_BLK, dtype=jnp.int32))
    total_rows = N_BLK * part_rows
    new_home = stacked[0].transpose(1, 0, 2).reshape(features, total_rows)
    new_home_state = stacked[1].reshape(total_rows)
    new_visit = jnp.roll(stacked[2], 1, axis=0).transpose(1, 0, 2).reshape(features, total_rows)
    new_visit_state = jnp.roll(stacked[3], 1, axis=0).reshape(total_rows)
    new_relation, new_relation_state = adagrad(relation_table, relation_state, relation_acc)
    return (new_home, new_home_state, new_visit, new_visit_state, new_relation, new_relation_state)
```

```python
import functools

import jax
import jax.numpy as jnp
from jax import lax
from jax.experimental import pallas as pl
from jax.experimental.pallas import tpu as pltpu
from jax.sharding import PartitionSpec as P

LEARN_RATE = 0.1
ADAGRAD_EPS = 1e-10
MESH = pl.DeviceIdType.MESH
LIVE = 1536
SHARE = 384
QROWS = 112
QPART = 50
QIM = 56
OWN_RELS = 29
VMEM = pl.BlockSpec(memory_space=pltpu.VMEM)
SMEM = pl.BlockSpec(memory_space=pltpu.SMEM)
NT = (((1,), (1,)), ((), ()))


def params(collective_id=None):
    if collective_id is None:
        return pltpu.CompilerParams(vmem_limit_bytes=56 * 2**20)
    return pltpu.CompilerParams(
        vmem_limit_bytes=56 * 2**20, collective_id=collective_id, has_side_effects=True
    )


def place():
    blk = lax.axis_index("blk")
    span = lax.axis_index("span")
    yh = lax.div(blk, 32)
    z = lax.rem(lax.div(blk, 4), 8)
    x = lax.rem(blk, 4)
    return yh, z, x, span


def device(yh, z, x, span):
    return (yh * 32 + lax.rem(z + 8, 8) * 4 + lax.rem(x + 4, 4), lax.rem(span, 4))


def remote(src, dst, send, recv, where):
    return pltpu.make_async_remote_copy(
        src_ref=src, dst_ref=dst, send_sem=send, recv_sem=recv, device_id=where, device_id_type=MESH
    )


def enter(peers):
    barrier = pltpu.get_barrier_semaphore()
    for peer in peers:
        pl.semaphore_signal(barrier, inc=1, device_id=peer, device_id_type=MESH)
    pl.semaphore_wait(barrier, len(peers))


def spread_kernel(
    piece_ref, low_ref, table_ref, low_all_ref, slots, p_send, p_recv, h_send, h_recv,
    y_send, y_recv, x_send, x_recv, r_send, r_recv, l_send, l_recv,
):
    yh, z, x, s = place()
    yo = 1 - yh
    span_peers = [device(yh, z, x, s + d) for d in (1, 2, 3)]
    x_peers = [device(yh, z, x + d, s) for d in (1, 2, 3)]
    y_peer = device(yo, z, x, s)
    right = device(yh, z + 1, x, s)
    left = device(yh, z - 1, x, s)
    enter(span_peers + x_peers + [y_peer, right, left])
    started = []

    def go(copy):
        copy.start()
        started.append(copy)
        return copy

    pieces = [
        go(remote(piece_ref.at[lax.rem(s + d, 4)], slots.at[d - 1], p_send.at[d - 1], p_recv.at[d - 1], span_peers[d - 1]))
        for d in (1, 2, 3)
    ]
    lows = [
        go(remote(low_ref, low_all_ref.at[s], h_send.at[d - 1], h_recv.at[d - 1], span_peers[d - 1]))
        for d in (1, 2, 3)
    ]
    low_all_ref[s] = low_ref[...]
    for copy in pieces:
        copy.wait_recv()
    table_ref[yh, z, x] = piece_ref[s] + slots[0] + slots[1] + slots[2]

    own = table_ref.at[yh, z, x]
    y_copy = go(remote(own, own, y_send, y_recv, y_peer))
    x_copies = [[], []]
    for d in (1, 2, 3):
        x_copies[0].append(go(remote(own, own, x_send.at[0, d - 1], x_recv.at[0, d - 1], x_peers[d - 1])))
    y_copy.wait_recv()
    other = table_ref.at[yo, z, x]
    for d in (1, 2, 3):
        x_copies[1].append(go(remote(other, other, x_send.at[1, d - 1], x_recv.at[1, d - 1], x_peers[d - 1])))

    def slab(chunk, zz):
        half = yh if chunk == 0 else yo
        return table_ref.at[half, lax.rem(zz + 8, 8)]

    steps = {("r", 0): 4, ("r", 1): 3, ("l", 0): 3, ("l", 1): 4}
    flying = {}
    for step in range(5):
        for chunk in (0, 1):
            if step == 0:
                for copy in x_copies[chunk]:
                    copy.wait_recv()
            for way in ("r", "l"):
                if 1 <= step <= steps[(way, chunk)]:
                    flying[(way, chunk, step - 1)].wait_recv()
                if step < steps[(way, chunk)]:
                    zz = z - step if way == "r" else z + step
                    send, recv = (r_send, r_recv) if way == "r" else (l_send, l_recv)
                    ref = slab(chunk, zz)
                    flying[(way, chunk, step)] = go(
                        remote(ref, ref, send.at[chunk, step], recv.at[chunk, step], right if way == "r" else left)
                    )
    for copy in lows:
        copy.wait_recv()
    for copy in started:
        copy.wait_send()


def spread(piece, low):
    dma = pltpu.SemaphoreType.DMA
    return pl.pallas_call(
        spread_kernel,
        out_shape=(
            jax.ShapeDtypeStruct((2, 8, 4, QROWS, 128), jnp.bfloat16),
            jax.ShapeDtypeStruct((4,) + low.shape, jnp.bfloat16),
        ),
        in_specs=[VMEM, VMEM],
        out_specs=(VMEM, VMEM),
        scratch_shapes=[
            pltpu.VMEM((3, QROWS, 128), jnp.bfloat16),
            dma((3,)), dma((3,)), dma((3,)), dma((3,)), dma, dma,
            dma((2, 3)), dma((2, 3)), dma((2, 4)), dma((2, 4)), dma((2, 4)), dma((2, 4)),
        ],
        compiler_params=params(0),
        name="spread",
    )(piece, low)


def one_hot(rows, index):
    row = lax.broadcasted_iota(jnp.int32, (rows, index.shape[1]), 0)
    return jnp.where(row == index, 1.0, 0.0).astype(jnp.bfloat16)


def pick_kernel(count_ref, index_ref, table_ref, slots_ref, picked_ref, low_hot, hot, total):
    at = lax.broadcasted_iota(jnp.int32, (8, LIVE), 1)
    kind = lax.broadcasted_iota(jnp.int32, (8, LIVE), 0)
    slots = jnp.full((8, LIVE), -1, jnp.int32)
    start = jnp.int32(0)
    for c in range(4):
        count = count_ref[c]
        listed = jnp.concatenate([index_ref[c], jnp.zeros((8, LIVE - 1024), jnp.int32)], axis=1)
        listed = pltpu.roll(listed, start, 1) + jnp.where(kind == 2, c * 256, 0)
        slots = jnp.where((at >= start) & (at < start + count), listed, slots)
        start = start + count
    slots = jnp.where(kind == 3, jnp.where(at < start, 1, 0), slots)
    slots_ref[...] = slots
    spot = slots[1:2]
    group = jnp.right_shift(spot, 7)
    low_hot[...] = one_hot(128, jnp.bitwise_and(spot, 127))
    total[...] = jnp.zeros_like(total)

    def chunk(i, carry):
        for k in range(8):
            mask = jnp.where(group == i * 8 + k, 1.0, 0.0).astype(jnp.bfloat16)
            hot[k * 128 : (k + 1) * 128, :] = low_hot[...] * mask
        block = jnp.concatenate([table_ref[i * 8 + k] for k in range(8)], axis=1)
        total[...] += jnp.dot(block, hot[...], preferred_element_type=jnp.float32)
        return carry

    lax.fori_loop(0, 8, chunk, 0)
    for c in range(4):
        picked_ref[c] = total[:, c * SHARE : (c + 1) * SHARE].astype(jnp.bfloat16)


def pick(counts, index, table):
    return pl.pallas_call(
        pick_kernel,
        out_shape=(
            jax.ShapeDtypeStruct((8, LIVE), jnp.int32),
            jax.ShapeDtypeStruct((4, QROWS, SHARE), jnp.bfloat16),
        ),
        in_specs=[SMEM, VMEM, VMEM],
        out_specs=(VMEM, VMEM),
        scratch_shapes=[
            pltpu.VMEM((128, LIVE), jnp.bfloat16),
            pltpu.VMEM((1024, LIVE), jnp.bfloat16),
            pltpu.VMEM((QROWS, LIVE), jnp.float32),
        ],
        compiler_params=params(),
        name="pick",
    )(counts, index, table)


def halves(value):
    high = value.astype(jnp.bfloat16)
    return high, (value - high.astype(jnp.float32)).astype(jnp.bfloat16)


def score_kernel(slots_ref, neg_ref, low_ref, rel_ref, rel_grad_ref, grads_ref):
    home = jnp.concatenate([low_ref[c, 0] for c in range(4)], axis=1)
    visit = jnp.concatenate([low_ref[c, 1] for c in range(4)], axis=1)
    live = slots_ref[3:4, :].astype(jnp.float32)
    hot_source = one_hot(1024, slots_ref[0:1, :])
    hot_dest = one_hot(1024, slots_ref[2:3, :])
    hot_neg = one_hot(1024, neg_ref[...])
    f32 = jnp.float32
    source = jnp.dot(home, hot_source, preferred_element_type=f32)
    dest = jnp.dot(visit, hot_dest, preferred_element_type=f32)
    negatives = jnp.dot(home, hot_neg, preferred_element_type=f32).astype(jnp.bfloat16)
    rel = [rel_ref[c].astype(f32) for c in range(4)]
    rel_re = jnp.concatenate([part[:QPART] for part in rel], axis=0)
    rel_im = jnp.concatenate([part[QIM : QIM + QPART] for part in rel], axis=0)
    middle = dest.shape[0] // 2
    dest_re, dest_im = dest[:middle], dest[middle:]
    trans = jnp.concatenate(
        [rel_re * dest_re - rel_im * dest_im, rel_re * dest_im + rel_im * dest_re], axis=0
    ).astype(jnp.bfloat16)
    positive = jnp.sum(source * trans.astype(f32), axis=0, keepdims=True)
    score = lax.dot_general(
        negatives, trans, (((0,), (0,)), ((), ())), preferred_element_type=f32
    )
    pos_weight = -live * jax.nn.sigmoid(-positive)
    weight = (live * jax.nn.sigmoid(score) * (1.0 / 1024.0)).astype(jnp.bfloat16)
    pull = jnp.dot(negatives, weight, preferred_element_type=f32)
    grad = pos_weight * source + pull
    grad_re, grad_im = grad[:middle], grad[middle:]
    out_re = dest_re * grad_re + dest_im * grad_im
    out_im = dest_re * grad_im - dest_im * grad_re
    pad = jnp.zeros((QIM - QPART, SHARE), f32)
    for c in range(4):
        rows = slice(c * QPART, (c + 1) * QPART)
        rel_grad_ref[c] = jnp.concatenate([out_re[rows], pad, out_im[rows], pad], axis=0)
    grad_dest = jnp.concatenate(
        [rel_re * grad_re + rel_im * grad_im, rel_re * grad_im - rel_im * grad_re], axis=0
    )
    share = jnp.dot(hot_neg, weight, preferred_element_type=f32) + pos_weight * hot_source.astype(f32)
    share_high, share_low = halves(share)
    dest_high, dest_low = halves(grad_dest)
    home_grad = lax.dot_general(trans, share_high, NT, preferred_element_type=f32) + lax.dot_general(
        trans, share_low, NT, preferred_element_type=f32
    )
    visit_grad = lax.dot_general(dest_high, hot_dest, NT, preferred_element_type=f32) + lax.dot_general(
        dest_low, hot_dest, NT, preferred_element_type=f32
    )
    for c in range(4):
        grads_ref[c, 0] = home_grad[:, c * 256 : (c + 1) * 256]
        grads_ref[c, 1] = visit_grad[:, c * 256 : (c + 1) * 256]


def score_slots(slots, neg_rows, low_all, rel):
    return pl.pallas_call(
        score_kernel,
        out_shape=(
            jax.ShapeDtypeStruct((4, QROWS, SHARE), jnp.float32),
            jax.ShapeDtypeStruct(low_all.shape, jnp.float32),
        ),
        in_specs=[VMEM] * 4,
        out_specs=(VMEM, VMEM),
        compiler_params=params(),
        name="score",
    )(slots, neg_rows, low_all, rel)


def put_kernel(slots_ref, grad_ref, out_ref, low_hot, hot, both):
    spot = slots_ref[1:2, :]
    group = jnp.right_shift(spot, 7)
    low_hot[...] = one_hot(128, jnp.bitwise_and(spot, 127))
    for c in range(4):
        high, low = halves(grad_ref[c])
        both[:QROWS, c * SHARE : (c + 1) * SHARE] = high
        both[QROWS:, c * SHARE : (c + 1) * SHARE] = low

    def chunk(i, carry):
        for k in range(8):
            mask = jnp.where(group == i * 8 + k, 1.0, 0.0).astype(jnp.bfloat16)
            hot[k * 128 : (k + 1) * 128, :] = low_hot[...] * mask
        sums = lax.dot_general(both[...], hot[...], NT, preferred_element_type=jnp.float32)
        sums = sums[:QROWS] + sums[QROWS:]
        for k in range(8):
            out_ref[i * 8 + k] = sums[:, k * 128 : (k + 1) * 128]
        return carry

    lax.fori_loop(0, 8, chunk, 0)


def put(slots, grad):
    return pl.pallas_call(
        put_kernel,
        out_shape=jax.ShapeDtypeStruct((64, QROWS, 128), jnp.float32),
        in_specs=[VMEM, VMEM],
        out_specs=VMEM,
        scratch_shapes=[
            pltpu.VMEM((128, LIVE), jnp.bfloat16),
            pltpu.VMEM((1024, LIVE), jnp.bfloat16),
            pltpu.VMEM((2 * QROWS, LIVE), jnp.bfloat16),
        ],
        compiler_params=params(),
        name="put",
    )(slots, grad)


def collect_kernel(
    rel_ref, grads_ref, rel_out_ref, grads_out_ref,
    r_buf, r_got, l_buf, l_got, total, x_got, x_sum, y_got, y_sum, m_got, o_buf, o_got,
    r_send, r_recv, l_send, l_recv, x_send, x_recv, y_send, y_recv, q_send, q_recv,
    m_send, m_recv, o_send, o_recv,
):
    yh, z, x, s = place()
    yo = 1 - yh
    span_peers = [device(yh, z, x, s + d) for d in (1, 2, 3)]
    x_peers = [device(yh, z, x + d, s) for d in (1, 2, 3)]
    y_peer = device(yo, z, x, s)
    right = device(yh, z + 1, x, s)
    left = device(yh, z - 1, x, s)
    mate_span = lax.div(s, 2) * 2 + 1 - lax.rem(s, 2)
    mate = device(yh, z, x, mate_span)
    across_span = lax.rem(s + 2, 4)
    across = device(yh, z, x, across_span)
    across_mate = lax.rem(mate_span + 2, 4)
    enter(span_peers + x_peers + [y_peer, right, left])
    started = []

    def go(copy):
        copy.start()
        started.append(copy)
        return copy

    far = {("r", 0): 4, ("r", 1): 3, ("l", 0): 3, ("l", 1): 4}
    flying = {}

    def ring(dist):
        for chunk in (0, 1):
            for way in ("r", "l"):
                if dist > far[(way, chunk)]:
                    continue
                buf, got, send, recv = (
                    (r_buf, r_got, r_send, r_recv) if way == "r" else (l_buf, l_got, l_send, l_recv)
                )
                zz = z + dist if way == "r" else z - dist
                value = rel_ref[chunk, lax.rem(zz + 8, 8)]
                if dist < far[(way, chunk)]:
                    flying[(way, chunk, dist + 1)].wait_recv()
                    value = value + got[chunk, dist].astype(jnp.float32)
                buf[chunk, dist - 1] = value.astype(jnp.bfloat16)
                flying[(way, chunk, dist)] = go(
                    remote(
                        buf.at[chunk, dist - 1], got.at[chunk, dist - 1],
                        send.at[chunk, dist - 1], recv.at[chunk, dist - 1],
                        right if way == "r" else left,
                    )
                )

    ring(4)
    m_copies = []
    for k in (1, 0):
        m_copies.append(go(remote(grads_ref.at[across_mate, k], m_got.at[1, k], m_send.at[1, k], m_recv.at[1, k], mate)))
    for k in (1, 0):
        m_copies.append(go(remote(grads_ref.at[mate_span, k], m_got.at[0, k], m_send.at[0, k], m_recv.at[0, k], mate)))
    ring(3)
    o_copies = []
    for i, k in enumerate((1, 0)):
        m_copies[i].wait_recv()
        o_buf[k] = grads_ref[across_span, k] + m_got[1, k]
        o_copies.append(go(remote(o_buf.at[k], o_got.at[k], o_send.at[k], o_recv.at[k], across)))
    ring(2)
    ring(1)
    x_copies = []
    for chunk in (0, 1):
        flying[("r", chunk, 1)].wait_recv()
        flying[("l", chunk, 1)].wait_recv()
        total[chunk] = (
            rel_ref[chunk, z] + r_got[chunk, 0].astype(jnp.float32) + l_got[chunk, 0].astype(jnp.float32)
        )
        for d in (1, 2, 3):
            x_copies.append(
                go(
                    remote(
                        total.at[chunk, lax.rem(x + d, 4)], x_got.at[chunk, d - 1],
                        x_send.at[chunk, d - 1], x_recv.at[chunk, d - 1], x_peers[d - 1],
                    )
                )
            )
    for copy in x_copies:
        copy.wait_recv()
    for chunk in (0, 1):
        x_sum[chunk] = total[chunk, x] + x_got[chunk, 0] + x_got[chunk, 1] + x_got[chunk, 2]
    y_copy = go(remote(x_sum.at[yo], y_got, y_send, y_recv, y_peer))
    y_copy.wait_recv()
    rel_out_ref[s] = x_sum[yh] + y_got[...]
    q_copies = [
        go(remote(rel_out_ref.at[s], rel_out_ref.at[s], q_send.at[d - 1], q_recv.at[d - 1], span_peers[d - 1]))
        for d in (1, 2, 3)
    ]
    for i, k in enumerate((1, 0)):
        m_copies[2 + i].wait_recv()
        o_copies[i].wait_recv()
        grads_out_ref[k] = grads_ref[s, k] + m_got[0, k] + o_got[k]
    for copy in q_copies:
        copy.wait_recv()
    for copy in started:
        copy.wait_send()


def collect(rel, grads):
    dma = pltpu.SemaphoreType.DMA
    f32, bf16 = jnp.float32, jnp.bfloat16
    pair = grads.shape[1:]
    return pl.pallas_call(
        collect_kernel,
        out_shape=(
            jax.ShapeDtypeStruct((4, QROWS, 128), f32),
            jax.ShapeDtypeStruct(pair, f32),
        ),
        in_specs=[VMEM, VMEM],
        out_specs=(VMEM, VMEM),
        scratch_shapes=[
            pltpu.VMEM((2, 4, 4, QROWS, 128), bf16), pltpu.VMEM((2, 4, 4, QROWS, 128), bf16),
            pltpu.VMEM((2, 4, 4, QROWS, 128), bf16), pltpu.VMEM((2, 4, 4, QROWS, 128), bf16),
            pltpu.VMEM((2, 4, QROWS, 128), f32), pltpu.VMEM((2, 3, QROWS, 128), f32),
            pltpu.VMEM((2, QROWS, 128), f32), pltpu.VMEM((QROWS, 128), f32), pltpu.VMEM((QROWS, 128), f32),
            pltpu.VMEM((2,) + pair, f32), pltpu.VMEM(pair, f32), pltpu.VMEM(pair, f32),
            dma((2, 4)), dma((2, 4)), dma((2, 4)), dma((2, 4)), dma((2, 3)), dma((2, 3)),
            dma, dma, dma((3,)), dma((3,)), dma((2, 2)), dma((2, 2)), dma((2,)), dma((2,)),
        ],
        compiler_params=params(1),
        name="collect",
    )(rel, grads)


def adagrad(table, state, grad_in):
    state_new = state + jnp.mean(grad_in * grad_in, axis=0)
    return (table - LEARN_RATE * grad_in / (jnp.sqrt(state_new)[None, :] + ADAGRAD_EPS), state_new)


def passed_along(value, axis, steps):
    count = lax.axis_size(axis)
    pairs = [(source, (source + steps) % count) for source in range(count)]
    return lax.ppermute(value, axis, pairs)


def shards(
    home_table, home_state, visit_table, visit_state, relation_table, relation_state,
    edge_src, edge_rel, edge_dst, edge_count, neg_rows,
):
    span = lax.axis_index("span")
    bf16 = jnp.bfloat16
    rel_spot = edge_rel[0, 0] // OWN_RELS * 32 + edge_rel[0, 0] % OWN_RELS
    index = jnp.stack(
        [edge_src[0, 0], rel_spot, edge_dst[0, 0], jnp.broadcast_to(edge_count[0, 0], rel_spot.shape)]
        + [jnp.zeros_like(rel_spot)] * 4
    )
    index = lax.all_gather(index, "span", axis=0)
    counts = index[:, 3, 0]
    quarters = relation_table.astype(bf16).reshape(2, 4, QPART, OWN_RELS).transpose(1, 0, 2, 3)
    quarters = jnp.pad(quarters, ((0, 0), (0, 0), (0, QIM - QPART), (0, 32 - OWN_RELS)))
    quarters = quarters.reshape(4, QROWS, 32)
    piece = lax.dynamic_update_slice(jnp.zeros((4, QROWS, 128), bf16), quarters, (0, 0, span * 32))
    low = jnp.stack([home_table, visit_table]).astype(bf16)
    table, low_all = spread(piece, low)
    slots, picked = pick(counts, index, table.reshape(64, QROWS, 128))
    rel = lax.all_to_all(picked, "span", 0, 0, tiled=True)
    own_slots = lax.dynamic_slice(slots, (0, span * SHARE), (8, SHARE))
    rel_grad, grads = score_slots(own_slots, neg_rows, low_all, rel)
    rel_grad = lax.all_to_all(rel_grad, "span", 0, 0, tiled=True)
    rel_all = put(slots, rel_grad).reshape(2, 8, 4, QROWS, 128)
    rel_sum, hv_sum = collect(rel_all, grads)
    visit_updated, visit_state_updated = adagrad(visit_table, visit_state, hv_sum[1])
    moved_table, moved_state = passed_along((visit_updated, visit_state_updated), "blk", 1)
    new_home, new_home_state = adagrad(home_table, home_state, hv_sum[0])
    own = lax.dynamic_slice(rel_sum, (0, 0, span * 32), (4, QROWS, 32))[:, :, :OWN_RELS]
    own = own.reshape(4, 2, QIM, OWN_RELS)[:, :, :QPART].transpose(1, 0, 2, 3)
    new_relation, new_relation_state = adagrad(
        relation_table, relation_state, own.reshape(8 * QPART, OWN_RELS)
    )
    return (new_home, new_home_state, moved_table, moved_state, new_relation, new_relation_state)


def solution(mesh):
    cols = P(None, ("blk", "span"))
    rows = P(("blk", "span"))
    slot = P("blk", "span", None)
    return jax.shard_map(
        shards,
        mesh=mesh,
        in_specs=(cols, rows, cols, rows, cols, rows, slot, slot, slot, P("blk", "span"), P("blk", None)),
        out_specs=(cols, rows, cols, rows, cols, rows),
        check_vma=False,
    )
```

```python
import functools

import jax
import jax.numpy as jnp
from jax import lax
from jax.experimental import pallas as pl
from jax.experimental.pallas import tpu as pltpu
from jax.sharding import PartitionSpec as P

LEARN_RATE = 0.1
ADAGRAD_EPS = 1e-10
MESH = pl.DeviceIdType.MESH
LIVE = 1536
SHARE = 384
QROWS = 112
QPART = 50
QIM = 56
OWN_RELS = 29
VMEM = pl.BlockSpec(memory_space=pltpu.VMEM)
SMEM = pl.BlockSpec(memory_space=pltpu.SMEM)
NT = (((1,), (1,)), ((), ()))


def params(collective_id=None):
    if collective_id is None:
        return pltpu.CompilerParams(vmem_limit_bytes=56 * 2**20)
    return pltpu.CompilerParams(
        vmem_limit_bytes=56 * 2**20, collective_id=collective_id, has_side_effects=True
    )


def place():
    blk = lax.axis_index("blk")
    span = lax.axis_index("span")
    yh = lax.div(blk, 32)
    z = lax.rem(lax.div(blk, 4), 8)
    x = lax.rem(blk, 4)
    return yh, z, x, span


def device(yh, z, x, span):
    return (yh * 32 + lax.rem(z + 8, 8) * 4 + lax.rem(x + 4, 4), lax.rem(span, 4))


def remote(src, dst, send, recv, where):
    return pltpu.make_async_remote_copy(
        src_ref=src, dst_ref=dst, send_sem=send, recv_sem=recv, device_id=where, device_id_type=MESH
    )


def greet(peers):
    barrier = pltpu.get_barrier_semaphore()
    for peer in peers:
        pl.semaphore_signal(barrier, inc=1, device_id=peer, device_id_type=MESH)


def greeted(peers):
    pl.semaphore_wait(pltpu.get_barrier_semaphore(), len(peers))


def one_hot(rows, index):
    row = lax.broadcasted_iota(jnp.int32, (rows, index.shape[1]), 0)
    return jnp.where(row == index, 1.0, 0.0).astype(jnp.bfloat16)


def halves(value):
    high = value.astype(jnp.bfloat16)
    return high, (value - high.astype(jnp.float32)).astype(jnp.bfloat16)


def hot_lanes(low_hot, hot, group, first):
    for k in range(4):
        mask = jnp.where(group == first + k, 1.0, 0.0).astype(jnp.bfloat16)
        hot[k * 128 : (k + 1) * 128, :] = low_hot[...] * mask


FAR = {("r", 0): 4, ("r", 1): 3, ("l", 0): 3, ("l", 1): 4}


def gather_kernel(
    src_ref, spot_ref, dst_ref, count_ref, home_ref, visit_ref, relation_ref,
    slots_ref, low_all_ref, picked_ref,
    low, piece, got_piece, index, table, low_hot, hot, total, mine,
    i_send, i_recv, p_send, p_recv, h_send, h_recv, y_send, y_recv, x_send, x_recv,
    r_send, r_recv, l_send, l_recv, q_send, q_recv,
):
    f32, bf16 = jnp.float32, jnp.bfloat16
    yh, z, x, s = place()
    yo = 1 - yh
    span_peers = [device(yh, z, x, s + d) for d in (1, 2, 3)]
    x_peers = [device(yh, z, x + d, s) for d in (1, 2, 3)]
    y_peer = device(yo, z, x, s)
    right = device(yh, z + 1, x, s)
    left = device(yh, z - 1, x, s)
    peers = span_peers + x_peers + [y_peer, right, left]
    greet(peers)

    low[0] = home_ref[...].astype(bf16)
    low[1] = visit_ref[...].astype(bf16)
    low_all_ref[s] = low[...]
    index[s] = jnp.concatenate(
        [
            src_ref[...],
            spot_ref[...],
            dst_ref[...] + s * 256,
            jnp.broadcast_to(count_ref[...], (1, 1024)),
            jnp.zeros((4, 1024), jnp.int32),
        ],
        axis=0,
    )
    operators = relation_ref[...]
    middle = operators.shape[0] // 2
    for c in range(4):
        re = operators[c * QPART : (c + 1) * QPART]
        im = operators[middle + c * QPART : middle + (c + 1) * QPART]
        pad = jnp.zeros((QIM - QPART, OWN_RELS), f32)
        quarter = jnp.concatenate([re, pad, im, pad], axis=0)
        placed = jnp.zeros((QROWS, 128), f32)
        for k in range(4):
            parts = [quarter, jnp.zeros((QROWS, 128 - 32 * k - OWN_RELS), f32)]
            if k:
                parts = [jnp.zeros((QROWS, 32 * k), f32)] + parts
            placed = jnp.where(s == k, jnp.concatenate(parts, axis=1), placed)
        piece[c] = placed.astype(bf16)
    greeted(peers)
    started = []

    def go(copy):
        copy.start()
        started.append(copy)
        return copy

    pieces = [
        go(remote(piece.at[lax.rem(s + d, 4)], got_piece.at[d - 1], p_send.at[d - 1], p_recv.at[d - 1], span_peers[d - 1]))
        for d in (1, 2, 3)
    ]
    lists = [
        go(remote(index.at[s], index.at[s], i_send.at[d - 1], i_recv.at[d - 1], span_peers[d - 1]))
        for d in (1, 2, 3)
    ]
    for copy in pieces:
        copy.wait_recv()
    table[yh, z, x] = piece[s] + got_piece[0] + got_piece[1] + got_piece[2]

    own = table.at[yh, z, x]
    other = table.at[yo, z, x]
    y_copy = go(remote(own, own, y_send, y_recv, y_peer))
    x_copies = [[], []]
    for d in (1, 2, 3):
        x_copies[0].append(go(remote(own, own, x_send.at[0, d - 1], x_recv.at[0, d - 1], x_peers[d - 1])))
    for copy in lists:
        copy.wait_recv()
    y_copy.wait_recv()
    for d in (1, 2, 3):
        x_copies[1].append(go(remote(other, other, x_send.at[1, d - 1], x_recv.at[1, d - 1], x_peers[d - 1])))

    at = lax.broadcasted_iota(jnp.int32, (8, LIVE), 1)
    kind = lax.broadcasted_iota(jnp.int32, (8, LIVE), 0)
    slots = jnp.full((8, LIVE), -1, jnp.int32)
    start = jnp.zeros((1, 1), jnp.int32)
    for c in range(4):
        part = index[c]
        end = start + part[3:4, 0:1]
        listed = jnp.concatenate([part, jnp.zeros((8, LIVE - 1024), jnp.int32)], axis=1)
        if c:
            for bit in range(11):
                on = jnp.bitwise_and(jnp.right_shift(start, bit), 1) == 1
                listed = jnp.where(on, pltpu.roll(listed, 1 << bit, 1), listed)
        slots = jnp.where((at >= start) & (at < end), listed, slots)
        start = end
    slots = jnp.where(kind == 3, jnp.where(at < start, 1, 0), slots)
    slots_ref[...] = slots
    spot = slots[1:2]
    group = jnp.right_shift(spot, 7)
    low_hot[...] = one_hot(128, jnp.bitwise_and(spot, 127))
    total[...] = jnp.zeros_like(total)

    def half(chunk):
        return yh if chunk == 0 else yo

    def gather(chunk, zz):
        zz = lax.rem(zz + 8, 8)
        hot_lanes(low_hot, hot, group, half(chunk) * 32 + zz * 4)
        block = jnp.concatenate([table[half(chunk), zz, k] for k in range(4)], axis=1)
        total[...] += jnp.dot(block, hot[...], preferred_element_type=f32)

    flying = {}
    lows = []
    for step in range(5):
        for chunk in (0, 1):
            if step == 0:
                for copy in x_copies[chunk]:
                    copy.wait_recv()
            for way in ("r", "l"):
                if 1 <= step <= FAR[(way, chunk)]:
                    flying[(way, chunk, step - 1)].wait_recv()
                if step < FAR[(way, chunk)]:
                    zz = z - step if way == "r" else z + step
                    send, recv = (r_send, r_recv) if way == "r" else (l_send, l_recv)
                    ref = table.at[half(chunk), lax.rem(zz + 8, 8)]
                    flying[(way, chunk, step)] = go(
                        remote(ref, ref, send.at[chunk, step], recv.at[chunk, step], right if way == "r" else left)
                    )
            if step == 0:
                for d in (1, 2, 3):
                    lows.append(
                        go(
                            remote(
                                low.at[chunk], low_all_ref.at[s, chunk],
                                h_send.at[chunk, d - 1], h_recv.at[chunk, d - 1], span_peers[d - 1],
                            )
                        )
                    )
                gather(chunk, z)
            else:
                for way in ("r", "l"):
                    if step <= FAR[(way, chunk)]:
                        gather(chunk, z - step if way == "r" else z + step)
    for c in range(4):
        mine[c] = total[:, c * SHARE : (c + 1) * SHARE].astype(bf16)
    picks = [
        go(remote(mine.at[lax.rem(s + d, 4)], picked_ref.at[s], q_send.at[d - 1], q_recv.at[d - 1], span_peers[d - 1]))
        for d in (1, 2, 3)
    ]
    picked_ref[s] = mine[s]
    for copy in lows + picks:
        copy.wait_recv()
    for copy in started:
        copy.wait_send()


def gather_all(src, spot, dst, count, home, visit, relation):
    dma = pltpu.SemaphoreType.DMA
    bf16, f32, i32 = jnp.bfloat16, jnp.float32, jnp.int32
    pair = (2,) + home.shape
    quarters = (4, QROWS, SHARE)
    return pl.pallas_call(
        gather_kernel,
        out_shape=(
            jax.ShapeDtypeStruct((8, LIVE), i32),
            jax.ShapeDtypeStruct((4,) + pair, bf16),
            jax.ShapeDtypeStruct(quarters, bf16),
        ),
        in_specs=[VMEM] * 7,
        out_specs=(VMEM,) * 3,
        scratch_shapes=[
            pltpu.VMEM(pair, bf16), pltpu.VMEM((4, QROWS, 128), bf16), pltpu.VMEM((3, QROWS, 128), bf16),
            pltpu.VMEM((4, 8, 1024), i32), pltpu.VMEM((2, 8, 4, QROWS, 128), bf16),
            pltpu.VMEM((128, LIVE), bf16), pltpu.VMEM((512, LIVE), bf16), pltpu.VMEM((QROWS, LIVE), f32),
            pltpu.VMEM(quarters, bf16),
            dma((3,)), dma((3,)), dma((3,)), dma((3,)), dma((2, 3)), dma((2, 3)), dma, dma,
            dma((2, 3)), dma((2, 3)), dma((2, 4)), dma((2, 4)), dma((2, 4)), dma((2, 4)), dma((3,)), dma((3,)),
        ],
        compiler_params=params(0),
        name="gather",
    )(src, spot, dst, count, home, visit, relation)


def adagrad(table, state, grad_in):
    state_new = state + jnp.sum(grad_in * grad_in, axis=0, keepdims=True) * (1.0 / grad_in.shape[0])
    return table - LEARN_RATE * grad_in / (jnp.sqrt(state_new) + ADAGRAD_EPS), state_new


def update_kernel(
    slots_ref, neg_ref, low_ref, rel_ref, home_ref, home_state_ref, visit_ref, visit_state_ref,
    relation_ref, relation_state_ref,
    home_out, home_state_out, visit_out, visit_state_out, relation_out, relation_state_out,
    rel_grad, rel_got, both, low_hot, hot, grads,
    r_buf, r_got, l_buf, l_got, total, x_got, x_sum, y_got, q_got, m_got, o_buf, o_got, moved, moved_state,
    a_send, a_recv, r_send, r_recv, l_send, l_recv, x_send, x_recv, y_send, y_recv, q_send, q_recv,
    m_send, m_recv, o_send, o_recv, v_send, v_recv,
):
    f32, bf16 = jnp.float32, jnp.bfloat16
    yh, z, x, s = place()
    yo = 1 - yh
    blk = lax.axis_index("blk")
    span_peers = [device(yh, z, x, s + d) for d in (1, 2, 3)]
    x_peers = [device(yh, z, x + d, s) for d in (1, 2, 3)]
    y_peer = device(yo, z, x, s)
    right = device(yh, z + 1, x, s)
    left = device(yh, z - 1, x, s)
    after = (lax.rem(blk + 1, 64), s)
    before = (lax.rem(blk + 63, 64), s)
    mate_span = lax.div(s, 2) * 2 + 1 - lax.rem(s, 2)
    mate = device(yh, z, x, mate_span)
    across_span = lax.rem(s + 2, 4)
    across = device(yh, z, x, across_span)
    across_mate = lax.rem(mate_span + 2, 4)
    peers = span_peers + x_peers + [y_peer, right, left, after, before]
    greet(peers)
    started = []

    def go(copy):
        copy.start()
        started.append(copy)
        return copy

    mine = slots_ref[:, pl.ds(pl.multiple_of(s * SHARE, 128), SHARE)]
    home = jnp.concatenate([low_ref[c, 0] for c in range(4)], axis=1)
    visit = jnp.concatenate([low_ref[c, 1] for c in range(4)], axis=1)
    live = mine[3:4, :].astype(f32)
    hot_source = one_hot(1024, mine[0:1, :])
    hot_dest = one_hot(1024, mine[2:3, :])
    hot_neg = one_hot(1024, neg_ref[...])
    source = jnp.dot(home, hot_source, preferred_element_type=f32)
    dest = jnp.dot(visit, hot_dest, preferred_element_type=f32)
    negatives = jnp.dot(home, hot_neg, preferred_element_type=f32).astype(bf16)
    rel = [rel_ref[c].astype(f32) for c in range(4)]
    rel_re = jnp.concatenate([part[:QPART] for part in rel], axis=0)
    rel_im = jnp.concatenate([part[QIM : QIM + QPART] for part in rel], axis=0)
    middle = dest.shape[0] // 2
    dest_re, dest_im = dest[:middle], dest[middle:]
    trans = jnp.concatenate(
        [rel_re * dest_re - rel_im * dest_im, rel_re * dest_im + rel_im * dest_re], axis=0
    ).astype(bf16)
    positive = jnp.sum(source * trans.astype(f32), axis=0, keepdims=True)
    score = lax.dot_general(negatives, trans, (((0,), (0,)), ((), ())), preferred_element_type=f32)
    pos_weight = -live * jax.nn.sigmoid(-positive)
    weight = (live * jax.nn.sigmoid(score) * (1.0 / 1024.0)).astype(bf16)
    pull = jnp.dot(negatives, weight, preferred_element_type=f32)
    grad = pos_weight * source + pull
    grad_re, grad_im = grad[:middle], grad[middle:]
    out_re = dest_re * grad_re + dest_im * grad_im
    out_im = dest_re * grad_im - dest_im * grad_re
    pad = jnp.zeros((QIM - QPART, SHARE), f32)
    for c in range(4):
        rows = slice(c * QPART, (c + 1) * QPART)
        rel_grad[c] = jnp.concatenate([out_re[rows], pad, out_im[rows], pad], axis=0)
    greeted(peers)
    swaps = [
        go(remote(rel_grad.at[lax.rem(s + d, 4)], rel_got.at[s], a_send.at[d - 1], a_recv.at[d - 1], span_peers[d - 1]))
        for d in (1, 2, 3)
    ]
    rel_got[s] = rel_grad[s]
    grad_dest = jnp.concatenate(
        [rel_re * grad_re + rel_im * grad_im, rel_re * grad_im - rel_im * grad_re], axis=0
    )
    dest_high, dest_low = halves(grad_dest)
    visit_grad = lax.dot_general(dest_high, hot_dest, NT, preferred_element_type=f32) + lax.dot_general(
        dest_low, hot_dest, NT, preferred_element_type=f32
    )
    for c in range(4):
        grads[c, 1] = visit_grad[:, c * 256 : (c + 1) * 256]
    share = jnp.dot(hot_neg, weight, preferred_element_type=f32) + pos_weight * hot_source.astype(f32)
    share_high, share_low = halves(share)
    home_grad = lax.dot_general(trans, share_high, NT, preferred_element_type=f32) + lax.dot_general(
        trans, share_low, NT, preferred_element_type=f32
    )
    for c in range(4):
        grads[c, 0] = home_grad[:, c * 256 : (c + 1) * 256]

    spot = slots_ref[1:2, :]
    group = jnp.right_shift(spot, 7)
    low_hot[...] = one_hot(128, jnp.bitwise_and(spot, 127))
    for copy in swaps:
        copy.wait_recv()
    for c in range(4):
        high, low = halves(rel_got[c])
        both[:QROWS, c * SHARE : (c + 1) * SHARE] = high
        both[QROWS:, c * SHARE : (c + 1) * SHARE] = low

    def scatter(chunk, zz):
        hot_lanes(low_hot, hot, group, chunk * 32 + lax.rem(zz + 8, 8) * 4)
        sums = lax.dot_general(both[...], hot[...], NT, preferred_element_type=f32)
        sums = sums[:QROWS] + sums[QROWS:]
        return [sums[:, k * 128 : (k + 1) * 128] for k in range(4)]

    flying = {}

    def ring(dist):
        for chunk in (0, 1):
            for way in ("r", "l"):
                if dist > FAR[(way, chunk)]:
                    continue
                buf, got, send, recv = (
                    (r_buf, r_got, r_send, r_recv) if way == "r" else (l_buf, l_got, l_send, l_recv)
                )
                value = scatter(chunk, z + dist if way == "r" else z - dist)
                if dist < FAR[(way, chunk)]:
                    flying[(way, chunk, dist + 1)].wait_recv()
                    value = [v + got[chunk, dist, k].astype(f32) for k, v in enumerate(value)]
                for k in range(4):
                    buf[chunk, dist - 1, k] = value[k].astype(bf16)
                flying[(way, chunk, dist)] = go(
                    remote(
                        buf.at[chunk, dist - 1], got.at[chunk, dist - 1],
                        send.at[chunk, dist - 1], recv.at[chunk, dist - 1],
                        right if way == "r" else left,
                    )
                )

    ring(4)
    m_copies = {}
    for k in (1, 0):
        for i, row in ((1, across_mate), (0, mate_span)):
            m_copies[(i, k)] = go(remote(grads.at[row, k], m_got.at[i, k], m_send.at[i, k], m_recv.at[i, k], mate))
    ring(3)
    o_copies = {}

    def cross(k):
        m_copies[(1, k)].wait_recv()
        o_buf[k] = grads[across_span, k] + m_got[1, k]
        o_copies[k] = go(remote(o_buf.at[k], o_got.at[k], o_send.at[k], o_recv.at[k], across))

    def summed(k):
        m_copies[(0, k)].wait_recv()
        o_copies[k].wait_recv()
        return grads[s, k] + m_got[0, k] + o_got[k]

    cross(1)
    cross(0)
    ring(2)
    ring(1)
    table, state = adagrad(visit_ref[...], visit_state_ref[...], summed(1))
    moved[...] = table
    moved_state[...] = jnp.broadcast_to(state, moved_state.shape)
    moves = [
        go(remote(moved, visit_out, v_send.at[0], v_recv.at[0], after)),
        go(remote(moved_state, visit_state_out, v_send.at[1], v_recv.at[1], after)),
    ]
    x_copies = []
    for chunk in (0, 1):
        own = scatter(chunk, z)
        flying[("r", chunk, 1)].wait_recv()
        flying[("l", chunk, 1)].wait_recv()
        for k in range(4):
            total[chunk, k] = own[k] + r_got[chunk, 0, k].astype(f32) + l_got[chunk, 0, k].astype(f32)
        for d in (1, 2, 3):
            x_copies.append(
                go(
                    remote(
                        total.at[chunk, lax.rem(x + d, 4)], x_got.at[chunk, d - 1],
                        x_send.at[chunk, d - 1], x_recv.at[chunk, d - 1], x_peers[d - 1],
                    )
                )
            )
    for copy in x_copies:
        copy.wait_recv()
    for chunk in (0, 1):
        x_sum[chunk] = total[chunk, x] + x_got[chunk, 0] + x_got[chunk, 1] + x_got[chunk, 2]
    y_copy = go(remote(x_sum.at[yo], y_got, y_send, y_recv, y_peer))
    home_new, home_state_new = adagrad(home_ref[...], home_state_ref[...], summed(0))
    home_out[...] = home_new
    home_state_out[...] = home_state_new
    y_copy.wait_recv()
    q_got[s] = x_sum[yh] + y_got[...]
    quarters = [
        go(remote(q_got.at[s], q_got.at[s], q_send.at[d - 1], q_recv.at[d - 1], span_peers[d - 1]))
        for d in (1, 2, 3)
    ]
    for copy in quarters:
        copy.wait_recv()
    res, ims = [], []
    for c in range(4):
        part = q_got[c]
        own = jnp.zeros((QROWS, OWN_RELS), f32)
        for k in range(4):
            own = jnp.where(s == k, part[:, 32 * k : 32 * k + OWN_RELS], own)
        res.append(own[:QPART])
        ims.append(own[QIM : QIM + QPART])
    table, state = adagrad(relation_ref[...], relation_state_ref[...], jnp.concatenate(res + ims, axis=0))
    relation_out[...] = table
    relation_state_out[...] = state
    for copy in moves:
        copy.wait_recv()
    for copy in started:
        copy.wait_send()


def update_all(slots, neg_rows, low_all, rel, home, home_state, visit, visit_state, relation, relation_state):
    dma = pltpu.SemaphoreType.DMA
    f32, bf16 = jnp.float32, jnp.bfloat16
    pair = (2,) + home.shape
    ring = pltpu.VMEM((2, 4, 4, QROWS, 128), bf16)
    return pl.pallas_call(
        update_kernel,
        out_shape=(
            jax.ShapeDtypeStruct(home.shape, f32),
            jax.ShapeDtypeStruct(home_state.shape, f32),
            jax.ShapeDtypeStruct(visit.shape, f32),
            jax.ShapeDtypeStruct((8, visit.shape[1]), f32),
            jax.ShapeDtypeStruct(relation.shape, f32),
            jax.ShapeDtypeStruct(relation_state.shape, f32),
        ),
        in_specs=[VMEM] * 10,
        out_specs=(VMEM,) * 6,
        scratch_shapes=[
            pltpu.VMEM((4, QROWS, SHARE), f32), pltpu.VMEM((4, QROWS, SHARE), f32),
            pltpu.VMEM((2 * QROWS, LIVE), bf16), pltpu.VMEM((128, LIVE), bf16), pltpu.VMEM((512, LIVE), bf16),
            pltpu.VMEM((4,) + pair, f32),
            ring, ring, ring, ring,
            pltpu.VMEM((2, 4, QROWS, 128), f32), pltpu.VMEM((2, 3, QROWS, 128), f32),
            pltpu.VMEM((2, QROWS, 128), f32), pltpu.VMEM((QROWS, 128), f32), pltpu.VMEM((4, QROWS, 128), f32),
            pltpu.VMEM((2,) + pair, f32), pltpu.VMEM(pair, f32), pltpu.VMEM(pair, f32),
            pltpu.VMEM(visit.shape, f32), pltpu.VMEM((8, visit.shape[1]), f32),
            dma((3,)), dma((3,)), dma((2, 4)), dma((2, 4)), dma((2, 4)), dma((2, 4)), dma((2, 3)), dma((2, 3)),
            dma, dma, dma((3,)), dma((3,)), dma((2, 2)), dma((2, 2)), dma((2,)), dma((2,)), dma((2,)), dma((2,)),
        ],
        compiler_params=params(1),
        name="update",
    )(slots, neg_rows, low_all, rel, home, home_state, visit, visit_state, relation, relation_state)


def shards(
    home_table, home_state, visit_table, visit_state, relation_table, relation_state,
    edge_src, edge_rel, edge_dst, edge_count, neg_rows,
):
    spot = edge_rel[0] // OWN_RELS * 32 + edge_rel[0] % OWN_RELS
    slots, low_all, rel = gather_all(
        edge_src[0], spot, edge_dst[0], edge_count, home_table, visit_table, relation_table
    )
    new_home, new_home_state, moved, moved_state, new_relation, new_relation_state = update_all(
        slots, neg_rows, low_all, rel, home_table, home_state[None], visit_table, visit_state[None],
        relation_table, relation_state[None],
    )
    return (new_home, new_home_state[0], moved, moved_state[0], new_relation, new_relation_state[0])


def solution(mesh):
    cols = P(None, ("blk", "span"))
    rows = P(("blk", "span"))
    slot = P("blk", "span", None)
    return jax.shard_map(
        shards,
        mesh=mesh,
        in_specs=(cols, rows, cols, rows, cols, rows, slot, slot, slot, P("blk", "span"), P("blk", None)),
        out_specs=(cols, rows, cols, rows, cols, rows),
        check_vma=False,
    )
```

```python
import functools

import jax
import jax.numpy as jnp
from jax import lax
from jax.experimental import pallas as pl
from jax.experimental.pallas import tpu as pltpu
from jax.sharding import PartitionSpec as P

LEARN_RATE = 0.1
ADAGRAD_EPS = 1e-10
MESH = pl.DeviceIdType.MESH
LIVE = 1536
SHARE = 384
QROWS = 112
QPART = 50
QIM = 56
OWN_RELS = 29
VMEM = pl.BlockSpec(memory_space=pltpu.VMEM)
SMEM = pl.BlockSpec(memory_space=pltpu.SMEM)
NT = (((1,), (1,)), ((), ()))


def params(collective_id=None):
    if collective_id is None:
        return pltpu.CompilerParams(vmem_limit_bytes=56 * 2**20)
    return pltpu.CompilerParams(
        vmem_limit_bytes=56 * 2**20, collective_id=collective_id, has_side_effects=True
    )


def place():
    blk = lax.axis_index("blk")
    span = lax.axis_index("span")
    yh = lax.div(blk, 32)
    z = lax.rem(lax.div(blk, 4), 8)
    x = lax.rem(blk, 4)
    return yh, z, x, span


def device(yh, z, x, span):
    return (yh * 32 + lax.rem(z + 8, 8) * 4 + lax.rem(x + 4, 4), lax.rem(span, 4))


def remote(src, dst, send, recv, where):
    return pltpu.make_async_remote_copy(
        src_ref=src, dst_ref=dst, send_sem=send, recv_sem=recv, device_id=where, device_id_type=MESH
    )


def greet(peers):
    barrier = pltpu.get_barrier_semaphore()
    for peer in peers:
        pl.semaphore_signal(barrier, inc=1, device_id=peer, device_id_type=MESH)


def greeted(peers):
    pl.semaphore_wait(pltpu.get_barrier_semaphore(), len(peers))


def one_hot(rows, index):
    row = lax.broadcasted_iota(jnp.int32, (rows, index.shape[1]), 0)
    return jnp.where(row == index, 1.0, 0.0).astype(jnp.bfloat16)


def halves(value):
    high = value.astype(jnp.bfloat16)
    return high, (value - high.astype(jnp.float32)).astype(jnp.bfloat16)


def hot_lanes(low_hot, hot, group, first):
    for k in range(4):
        mask = jnp.where(group == first + k, 1.0, 0.0).astype(jnp.bfloat16)
        hot[k * 128 : (k + 1) * 128, :] = low_hot[...] * mask


FAR = {("r", 0): 4, ("r", 1): 3, ("l", 0): 3, ("l", 1): 4}


def round_kernel(
    src_ref, rel_ref, dst_ref, count_ref, neg_ref, home_ref, visit_ref, visit_state_ref, relation_ref,
    home_grad_ref, visit_out, visit_state_out, visit_grad_ref, quarter_ref,
    low, low_all, piece, got_piece, index, table, low_hot, hot, total, mine, picked,
    hot_neg, negatives, rel_grad, rel_got, both, grads,
    r_buf, r_got, l_buf, l_got, row_sum, x_got, x_sum, y_got, m_got, o_buf, o_got, visit_sum,
    i_send, i_recv, p_send, p_recv, h_send, h_recv, y_send, y_recv, x_send, x_recv,
    r_send, r_recv, l_send, l_recv, k_send, k_recv, v_send, v_recv, a_send, a_recv,
    rr_send, rr_recv, ll_send, ll_recv, xx_send, xx_recv, yy_send, yy_recv, q_send, q_recv,
    m_send, m_recv, o_send, o_recv,
):
    f32, bf16 = jnp.float32, jnp.bfloat16
    yh, z, x, s = place()
    yo = 1 - yh
    blk = lax.axis_index("blk")
    span_peers = [device(yh, z, x, s + d) for d in (1, 2, 3)]
    x_peers = [device(yh, z, x + d, s) for d in (1, 2, 3)]
    y_peer = device(yo, z, x, s)
    right = device(yh, z + 1, x, s)
    left = device(yh, z - 1, x, s)
    after = (lax.rem(blk + 1, 64), s)
    before = (lax.rem(blk + 63, 64), s)
    mate_span = lax.div(s, 2) * 2 + 1 - lax.rem(s, 2)
    mate = device(yh, z, x, mate_span)
    across_span = lax.rem(s + 2, 4)
    across = device(yh, z, x, across_span)
    across_mate = lax.rem(mate_span + 2, 4)
    peers = span_peers + x_peers + [y_peer, right, left, after, before]
    greet(peers)

    operators = jnp.concatenate([relation_ref[...], jnp.zeros((32 - OWN_RELS, 8 * QPART), f32)], axis=0).T
    middle = operators.shape[0] // 2
    pad = jnp.zeros((QIM - QPART, 32), f32)
    for c in range(4):
        re = operators[c * QPART : (c + 1) * QPART]
        im = operators[middle + c * QPART : middle + (c + 1) * QPART]
        quarter = jnp.concatenate([re, pad, im, pad], axis=0)
        placed = jnp.zeros((QROWS, 128), f32)
        for k in range(4):
            parts = [jnp.zeros((QROWS, 32), f32)] * 4
            parts[k] = quarter
            placed = jnp.where(s == k, jnp.concatenate(parts, axis=1), placed)
        piece[c] = placed.astype(bf16)
    rel = rel_ref[...]
    owner = jnp.right_shift(rel * 4520, 17)
    index[s] = jnp.concatenate(
        [
            src_ref[...],
            rel + owner * (32 - OWN_RELS),
            dst_ref[...] + s * 256,
            jnp.broadcast_to(count_ref[...], (1, 1024)),
            jnp.zeros((4, 1024), jnp.int32),
        ],
        axis=0,
    )
    low[0] = home_ref[...].astype(bf16)
    low[1] = visit_ref[...].astype(bf16)
    low_all[s] = low[...]
    greeted(peers)
    started = []

    def go(copy):
        copy.start()
        started.append(copy)
        return copy

    def to_span(src_of, dst, send, recv):
        return [
            go(remote(src_of(lax.rem(s + d, 4)), dst, send.at[d - 1], recv.at[d - 1], span_peers[d - 1]))
            for d in (1, 2, 3)
        ]

    pieces = [
        go(remote(piece.at[lax.rem(s + d, 4)], got_piece.at[d - 1], p_send.at[d - 1], p_recv.at[d - 1], span_peers[d - 1]))
        for d in (1, 2, 3)
    ]
    lists = to_span(lambda peer: index.at[s], index.at[s], i_send, i_recv)
    for copy in pieces:
        copy.wait_recv()
    table[yh, z, x] = piece[s] + got_piece[0] + got_piece[1] + got_piece[2]

    own = table.at[yh, z, x]
    other = table.at[yo, z, x]
    y_copy = go(remote(own, own, y_send, y_recv, y_peer))
    x_copies = [[], []]
    for d in (1, 2, 3):
        x_copies[0].append(go(remote(own, own, x_send.at[0, d - 1], x_recv.at[0, d - 1], x_peers[d - 1])))
    for copy in lists:
        copy.wait_recv()
    y_copy.wait_recv()
    for d in (1, 2, 3):
        x_copies[1].append(go(remote(other, other, x_send.at[1, d - 1], x_recv.at[1, d - 1], x_peers[d - 1])))

    at = lax.broadcasted_iota(jnp.int32, (8, LIVE), 1)
    kind = lax.broadcasted_iota(jnp.int32, (8, LIVE), 0)
    slots = jnp.full((8, LIVE), -1, jnp.int32)
    start = jnp.zeros((1, 1), jnp.int32)
    for c in range(4):
        part = index[c]
        end = start + part[3:4, 0:1]
        listed = jnp.concatenate([part, jnp.zeros((8, LIVE - 1024), jnp.int32)], axis=1)
        if c:
            for bit in range(11):
                on = jnp.bitwise_and(jnp.right_shift(start, bit), 1) == 1
                listed = jnp.where(on, pltpu.roll(listed, 1 << bit, 1), listed)
        slots = jnp.where((at >= start) & (at < end), listed, slots)
        start = end
    slots = jnp.where(kind == 3, jnp.where(at < start, 1, 0), slots)
    share_slots = jnp.zeros((8, SHARE), jnp.int32)
    for c in range(4):
        share_slots = jnp.where(s == c, slots[:, c * SHARE : (c + 1) * SHARE], share_slots)
    spot = slots[1:2]
    group = jnp.right_shift(spot, 7)
    low_hot[...] = one_hot(128, jnp.bitwise_and(spot, 127))
    total[...] = jnp.zeros_like(total)

    def half(chunk):
        return yh if chunk == 0 else yo

    def gather(chunk, zz):
        zz = lax.rem(zz + 8, 8)
        hot_lanes(low_hot, hot, group, half(chunk) * 32 + zz * 4)
        block = jnp.concatenate([table[half(chunk), zz, k] for k in range(4)], axis=1)
        total[...] += jnp.dot(block, hot[...], preferred_element_type=f32)

    flying = {}
    lows = [[], []]
    for step in range(5):
        for chunk in (0, 1):
            if step == 0:
                for copy in x_copies[chunk]:
                    copy.wait_recv()
            for way in ("r", "l"):
                if 1 <= step <= FAR[(way, chunk)]:
                    flying[(way, chunk, step - 1)].wait_recv()
                if step < FAR[(way, chunk)]:
                    zz = z - step if way == "r" else z + step
                    send, recv = (r_send, r_recv) if way == "r" else (l_send, l_recv)
                    ref = table.at[half(chunk), lax.rem(zz + 8, 8)]
                    flying[(way, chunk, step)] = go(
                        remote(ref, ref, send.at[chunk, step], recv.at[chunk, step], right if way == "r" else left)
                    )
            if step == 0:
                lows[chunk] = to_span(lambda peer: low.at[chunk], low_all.at[s, chunk], h_send.at[chunk], h_recv.at[chunk])
                gather(chunk, z)
            else:
                for way in ("r", "l"):
                    if step <= FAR[(way, chunk)]:
                        gather(chunk, z - step if way == "r" else z + step)
            if step == 3 and chunk == 0:
                for copy in lows[0]:
                    copy.wait_recv()
                hot_neg[...] = one_hot(1024, neg_ref[...])
            if step == 3 and chunk == 1:
                home = jnp.concatenate([low_all[c, 0] for c in range(4)], axis=1)
                negatives[...] = jnp.dot(home, hot_neg[...], preferred_element_type=f32).astype(bf16)
    for c in range(4):
        mine[c] = total[:, c * SHARE : (c + 1) * SHARE].astype(bf16)
    picks = to_span(lambda peer: mine.at[peer], picked.at[s], k_send, k_recv)
    picked[s] = mine[s]
    moves = [
        go(remote(visit_ref, visit_out, v_send.at[0], v_recv.at[0], after)),
        go(remote(visit_state_ref, visit_state_out, v_send.at[1], v_recv.at[1], after)),
    ]

    for copy in lows[1]:
        copy.wait_recv()
    visit = jnp.concatenate([low_all[c, 1] for c in range(4)], axis=1)
    live = share_slots[3:4, :].astype(f32)
    hot_source = one_hot(1024, share_slots[0:1, :])
    hot_dest = one_hot(1024, share_slots[2:3, :])
    source = jnp.dot(home, hot_source, preferred_element_type=f32)
    dest = jnp.dot(visit, hot_dest, preferred_element_type=f32)
    dest_re, dest_im = dest[:middle], dest[middle:]
    for copy in picks:
        copy.wait_recv()
    rel = [picked[c].astype(f32) for c in range(4)]
    rel_re = jnp.concatenate([part[:QPART] for part in rel], axis=0)
    rel_im = jnp.concatenate([part[QIM : QIM + QPART] for part in rel], axis=0)
    trans = jnp.concatenate(
        [rel_re * dest_re - rel_im * dest_im, rel_re * dest_im + rel_im * dest_re], axis=0
    ).astype(bf16)
    positive = jnp.sum(source * trans.astype(f32), axis=0, keepdims=True)
    score = lax.dot_general(negatives[...], trans, (((0,), (0,)), ((), ())), preferred_element_type=f32)
    pos_weight = -live * jax.nn.sigmoid(-positive)
    weight = (live * jax.nn.sigmoid(score) * (1.0 / 1024.0)).astype(bf16)
    pull = jnp.dot(negatives[...], weight, preferred_element_type=f32)
    grad = pos_weight * source + pull
    grad_re, grad_im = grad[:middle], grad[middle:]
    out_re = dest_re * grad_re + dest_im * grad_im
    out_im = dest_re * grad_im - dest_im * grad_re
    pad = jnp.zeros((QIM - QPART, SHARE), f32)
    for c in range(4):
        rows = slice(c * QPART, (c + 1) * QPART)
        rel_grad[c] = jnp.concatenate([out_re[rows], pad, out_im[rows], pad], axis=0)
    swaps = to_span(lambda peer: rel_grad.at[peer], rel_got.at[s], a_send, a_recv)
    rel_got[s] = rel_grad[s]
    grad_dest = jnp.concatenate(
        [rel_re * grad_re + rel_im * grad_im, rel_re * grad_im - rel_im * grad_re], axis=0
    )
    dest_high, dest_low = halves(grad_dest)
    visit_grad = lax.dot_general(dest_high, hot_dest, NT, preferred_element_type=f32) + lax.dot_general(
        dest_low, hot_dest, NT, preferred_element_type=f32
    )
    share = jnp.dot(hot_neg[...], weight, preferred_element_type=f32) + pos_weight * hot_source.astype(f32)
    share_high, share_low = halves(share)
    home_grad = lax.dot_general(trans, share_high, NT, preferred_element_type=f32) + lax.dot_general(
        trans, share_low, NT, preferred_element_type=f32
    )
    for c in range(4):
        grads[c, 0] = home_grad[:, c * 256 : (c + 1) * 256]
        grads[c, 1] = visit_grad[:, c * 256 : (c + 1) * 256]

    for copy in swaps:
        copy.wait_recv()
    for c in range(4):
        high, rest = halves(rel_got[c])
        both[:QROWS, c * SHARE : (c + 1) * SHARE] = high
        both[QROWS:, c * SHARE : (c + 1) * SHARE] = rest

    def scatter(chunk, zz):
        hot_lanes(low_hot, hot, group, chunk * 32 + lax.rem(zz + 8, 8) * 4)
        sums = lax.dot_general(both[...], hot[...], NT, preferred_element_type=f32)
        sums = sums[:QROWS] + sums[QROWS:]
        return [sums[:, k * 128 : (k + 1) * 128] for k in range(4)]

    back = {}

    def ring(dist):
        for chunk in (0, 1):
            for way in ("r", "l"):
                if dist > FAR[(way, chunk)]:
                    continue
                buf, got, send, recv = (
                    (r_buf, r_got, rr_send, rr_recv) if way == "r" else (l_buf, l_got, ll_send, ll_recv)
                )
                value = scatter(chunk, z + dist if way == "r" else z - dist)
                if dist < FAR[(way, chunk)]:
                    back[(way, chunk, dist + 1)].wait_recv()
                    value = [v + got[chunk, dist, k].astype(f32) for k, v in enumerate(value)]
                for k in range(4):
                    buf[chunk, dist - 1, k] = value[k].astype(bf16)
                back[(way, chunk, dist)] = go(
                    remote(
                        buf.at[chunk, dist - 1], got.at[chunk, dist - 1],
                        send.at[chunk, dist - 1], recv.at[chunk, dist - 1],
                        right if way == "r" else left,
                    )
                )

    m_copies = {}
    o_copies = {}

    def to_mate(k):
        for i, row in ((1, across_mate), (0, mate_span)):
            m_copies[(i, k)] = go(remote(grads.at[row, k], m_got.at[i, k], m_send.at[i, k], m_recv.at[i, k], mate))

    def cross(k):
        m_copies[(1, k)].wait_recv()
        o_buf[k] = (grads[across_span, k] + m_got[1, k]).astype(bf16)
        o_copies[k] = go(remote(o_buf.at[k], o_got.at[k], o_send.at[k], o_recv.at[k], across))

    def summed(k):
        m_copies[(0, k)].wait_recv()
        o_copies[k].wait_recv()
        return grads[s, k] + m_got[0, k] + o_got[k].astype(f32)

    ring(4)
    to_mate(1)
    ring(3)
    to_mate(0)
    cross(1)
    ring(2)
    cross(0)
    visit_sum[...] = summed(1).astype(bf16)
    moves.append(go(remote(visit_sum, visit_grad_ref, v_send.at[2], v_recv.at[2], after)))
    ring(1)
    x_copies = []
    for chunk in (0, 1):
        near = scatter(chunk, z)
        back[("r", chunk, 1)].wait_recv()
        back[("l", chunk, 1)].wait_recv()
        for k in range(4):
            row_sum[chunk, k] = near[k] + r_got[chunk, 0, k].astype(f32) + l_got[chunk, 0, k].astype(f32)
        for d in (1, 2, 3):
            x_copies.append(
                go(
                    remote(
                        row_sum.at[chunk, lax.rem(x + d, 4)], x_got.at[chunk, d - 1],
                        xx_send.at[chunk, d - 1], xx_recv.at[chunk, d - 1], x_peers[d - 1],
                    )
                )
            )
    home_grad_ref[...] = summed(0)
    for copy in x_copies:
        copy.wait_recv()
    for chunk in (0, 1):
        x_sum[chunk] = row_sum[chunk, x] + x_got[chunk, 0] + x_got[chunk, 1] + x_got[chunk, 2]
    y_copy = go(remote(x_sum.at[yo], y_got, yy_send, yy_recv, y_peer))
    y_copy.wait_recv()
    quarter_ref[s] = x_sum[yh] + y_got[...]
    for copy in to_span(lambda peer: quarter_ref.at[s], quarter_ref.at[s], q_send, q_recv) + moves:
        copy.wait_recv()
    for copy in started:
        copy.wait_send()


def bucket_round(src, rel, dst, count, neg_rows, home, visit, visit_state, relation):
    dma = pltpu.SemaphoreType.DMA
    bf16, f32, i32 = jnp.bfloat16, jnp.float32, jnp.int32
    pair = (2,) + home.shape
    quarters = (4, QROWS, SHARE)
    ring = pltpu.VMEM((2, 4, 4, QROWS, 128), bf16)
    rows = home.shape[0]
    return pl.pallas_call(
        round_kernel,
        out_shape=(
            jax.ShapeDtypeStruct(home.shape, f32),
            jax.ShapeDtypeStruct(visit.shape, f32),
            jax.ShapeDtypeStruct(visit_state.shape, f32),
            jax.ShapeDtypeStruct(visit.shape, bf16),
            jax.ShapeDtypeStruct((4, QROWS, 128), f32),
        ),
        in_specs=[VMEM] * 9,
        out_specs=(VMEM,) * 5,
        scratch_shapes=[
            pltpu.VMEM(pair, bf16), pltpu.VMEM((4,) + pair, bf16),
            pltpu.VMEM((4, QROWS, 128), bf16), pltpu.VMEM((3, QROWS, 128), bf16),
            pltpu.VMEM((4, 8, 1024), i32), pltpu.VMEM((2, 8, 4, QROWS, 128), bf16),
            pltpu.VMEM((128, LIVE), bf16), pltpu.VMEM((512, LIVE), bf16), pltpu.VMEM((QROWS, LIVE), f32),
            pltpu.VMEM(quarters, bf16), pltpu.VMEM(quarters, bf16),
            pltpu.VMEM((1024, 1024), bf16), pltpu.VMEM((rows, 1024), bf16),
            pltpu.VMEM(quarters, f32), pltpu.VMEM(quarters, f32), pltpu.VMEM((2 * QROWS, LIVE), bf16),
            pltpu.VMEM((4,) + pair, f32),
            ring, ring, ring, ring,
            pltpu.VMEM((2, 4, QROWS, 128), f32), pltpu.VMEM((2, 3, QROWS, 128), f32),
            pltpu.VMEM((2, QROWS, 128), f32), pltpu.VMEM((QROWS, 128), f32),
            pltpu.VMEM((2,) + pair, f32), pltpu.VMEM(pair, bf16), pltpu.VMEM(pair, bf16),
            pltpu.VMEM(visit.shape, bf16),
            dma((3,)), dma((3,)), dma((3,)), dma((3,)), dma((2, 3)), dma((2, 3)), dma, dma,
            dma((2, 3)), dma((2, 3)), dma((2, 4)), dma((2, 4)), dma((2, 4)), dma((2, 4)),
            dma((3,)), dma((3,)), dma((3,)), dma((3,)), dma((3,)), dma((3,)),
            dma((2, 4)), dma((2, 4)), dma((2, 4)), dma((2, 4)), dma((2, 3)), dma((2, 3)),
            dma, dma, dma((3,)), dma((3,)), dma((2, 2)), dma((2, 2)), dma((2,)), dma((2,)),
        ],
        compiler_params=params(0),
        name="bucket_round",
    )(src, rel, dst, count, neg_rows, home, visit, visit_state, relation)


def adagrad(table, state, grad_in, axis):
    state_new = state + jnp.sum(grad_in * grad_in, axis=axis, keepdims=True) * (1.0 / grad_in.shape[axis])
    return table - LEARN_RATE * grad_in / (jnp.sqrt(state_new) + ADAGRAD_EPS), state_new


def update_kernel(
    home_grad_ref, home_ref, home_state_ref, visit_grad_ref, visit_ref, visit_state_ref,
    quarter_ref, relation_ref, relation_state_ref,
    home_out, home_state_out, visit_out, visit_state_out, relation_out, relation_state_out,
):
    f32 = jnp.float32
    s = lax.axis_index("span")
    home_out[...], home_state_out[...] = adagrad(home_ref[...], home_state_ref[...], home_grad_ref[...], 0)
    visit_out[...], visit_state_out[...] = adagrad(
        visit_ref[...], visit_state_ref[...], visit_grad_ref[...].astype(f32), 0
    )
    res, ims = [], []
    for c in range(4):
        part = quarter_ref[c]
        own = jnp.zeros((QROWS, 32), f32)
        for k in range(4):
            own = jnp.where(s == k, part[:, 32 * k : 32 * (k + 1)], own)
        res.append(own[:QPART])
        ims.append(own[QIM : QIM + QPART])
    grad = jnp.concatenate(res + ims, axis=0)
    state = relation_state_ref[...] + jnp.sum(grad * grad, axis=0, keepdims=True)[:, :OWN_RELS] * (1.0 / grad.shape[0])
    step = grad[:, :OWN_RELS] / (jnp.sqrt(state) + ADAGRAD_EPS)
    step = jnp.concatenate([step, jnp.zeros((grad.shape[0], 32 - OWN_RELS), f32)], axis=1).T[:OWN_RELS]
    relation_out[...] = relation_ref[...] - LEARN_RATE * step
    relation_state_out[...] = state


def update(*arrays):
    shape = lambda a: jax.ShapeDtypeStruct(a.shape, jnp.float32)
    return pl.pallas_call(
        update_kernel,
        out_shape=tuple(shape(arrays[i]) for i in (1, 2, 4, 5, 7, 8)),
        in_specs=[VMEM] * 9,
        out_specs=(VMEM,) * 6,
        compiler_params=params(),
        name="update",
    )(*arrays)


def shards(
    home_table, home_state, visit_table, visit_state, relation_table, relation_state,
    edge_src, edge_rel, edge_dst, edge_count, neg_rows,
):
    home_grad, moved, moved_state, moved_grad, quarters = bucket_round(
        edge_src[0], edge_rel[0], edge_dst[0], edge_count, neg_rows,
        home_table, visit_table, visit_state[None], relation_table.T,
    )
    new_home, new_home_state, new_visit, new_visit_state, new_relation, new_relation_state = update(
        home_grad, home_table, home_state[None], moved_grad, moved, moved_state,
        quarters, relation_table.T, relation_state[None],
    )
    return (new_home, new_home_state[0], new_visit, new_visit_state[0], new_relation.T, new_relation_state[0])


def solution(mesh):
    cols = P(None, ("blk", "span"))
    rows = P(("blk", "span"))
    slot = P("blk", "span", None)
    return jax.shard_map(
        shards,
        mesh=mesh,
        in_specs=(cols, rows, cols, rows, cols, rows, slot, slot, slot, P("blk", "span"), P("blk", None)),
        out_specs=(cols, rows, cols, rows, cols, rows),
        check_vma=False,
    )
```

```python
import functools

import jax
import jax.numpy as jnp
from jax import lax
from jax.experimental import pallas as pl
from jax.experimental.pallas import tpu as pltpu
from jax.sharding import PartitionSpec as P

LEARN_RATE = 0.1
ADAGRAD_EPS = 1e-10
MESH = pl.DeviceIdType.MESH
LIVE = 1536
SHARE = 384
QROWS = 112
QPART = 50
QIM = 56
OWN_RELS = 29
VMEM = pl.BlockSpec(memory_space=pltpu.VMEM)
SMEM = pl.BlockSpec(memory_space=pltpu.SMEM)
NT = (((1,), (1,)), ((), ()))


def params(collective_id=None):
    if collective_id is None:
        return pltpu.CompilerParams(vmem_limit_bytes=56 * 2**20)
    return pltpu.CompilerParams(
        vmem_limit_bytes=56 * 2**20, collective_id=collective_id, has_side_effects=True
    )


def place():
    blk = lax.axis_index("blk")
    span = lax.axis_index("span")
    yh = lax.div(blk, 32)
    z = lax.rem(lax.div(blk, 4), 8)
    x = lax.rem(blk, 4)
    return yh, z, x, span


def device(yh, z, x, span):
    return (yh * 32 + lax.rem(z + 8, 8) * 4 + lax.rem(x + 4, 4), lax.rem(span, 4))


def remote(src, dst, send, recv, where):
    return pltpu.make_async_remote_copy(
        src_ref=src, dst_ref=dst, send_sem=send, recv_sem=recv, device_id=where, device_id_type=MESH
    )


def greet(peers):
    barrier = pltpu.get_barrier_semaphore()
    for peer in peers:
        pl.semaphore_signal(barrier, inc=1, device_id=peer, device_id_type=MESH)


def greeted(peers):
    pl.semaphore_wait(pltpu.get_barrier_semaphore(), len(peers))


def one_hot(rows, index):
    row = lax.broadcasted_iota(jnp.int32, (rows, index.shape[1]), 0)
    return jnp.where(row == index, 1.0, 0.0).astype(jnp.bfloat16)


def halves(value):
    high = value.astype(jnp.bfloat16)
    return high, (value - high.astype(jnp.float32)).astype(jnp.bfloat16)


def hot_lanes(low_hot, hot, group, first):
    for k in range(4):
        mask = jnp.where(group == first + k, 1.0, 0.0).astype(jnp.bfloat16)
        hot[k * 128 : (k + 1) * 128, :] = low_hot[...] * mask


FAR = {("r", 0): 4, ("r", 1): 3, ("l", 0): 3, ("l", 1): 4}


def round_kernel(
    src_ref, rel_ref, dst_ref, count_ref, neg_ref, home_ref, visit_ref, visit_state_ref, relation_ref,
    home_grad_ref, visit_out, visit_state_out, visit_grad_ref, quarter_ref,
    low, low_all, piece, got_piece, index, table, low_hot, hot, total, mine, picked,
    hot_neg, negatives, rel_grad, rel_got, both, grads,
    r_buf, r_got, l_buf, l_got, row_sum, x_got, x_sum, y_got, q_buf, m_got, o_buf, o_got, visit_sum,
    negatives_t, kept, cast, x_in, one_buf, one_got,
    i_send, i_recv, p_send, p_recv, h_send, h_recv, y_send, y_recv, x_send, x_recv,
    r_send, r_recv, l_send, l_recv, k_send, k_recv, v_send, v_recv, a_send, a_recv,
    rr_send, rr_recv, ll_send, ll_recv, xx_send, xx_recv, yy_send, yy_recv, q_send, q_recv,
    m_send, m_recv, o_send, o_recv, b_send, b_recv, c_send, c_recv, w_send, w_recv,
    xb_send, xb_recv, e_send, e_recv,
):
    f32, bf16 = jnp.float32, jnp.bfloat16
    yh, z, x, s = place()
    yo = 1 - yh
    blk = lax.axis_index("blk")
    span_peers = [device(yh, z, x, s + d) for d in (1, 2, 3)]
    x_peers = [device(yh, z, x + d, s) for d in (1, 2, 3)]
    y_peer = device(yo, z, x, s)
    right = device(yh, z + 1, x, s)
    left = device(yh, z - 1, x, s)
    after = (lax.rem(blk + 1, 64), s)
    before = (lax.rem(blk + 63, 64), s)
    mate_span = lax.div(s, 2) * 2 + 1 - lax.rem(s, 2)
    mate = device(yh, z, x, mate_span)
    across_span = lax.rem(s + 2, 4)
    across = device(yh, z, x, across_span)
    across_mate = lax.rem(mate_span + 2, 4)
    peers = span_peers + x_peers + [y_peer, right, left, after, before]
    greet(peers)

    middle = 4 * QPART
    spare = jnp.zeros((32 - OWN_RELS, 2 * middle), f32)
    operators = jnp.concatenate([relation_ref[...], spare], axis=0)
    for c in range(4):
        re = operators[:, c * QPART : (c + 1) * QPART]
        im = operators[:, middle + c * QPART : middle + (c + 1) * QPART]
        pad = jnp.zeros((32, QIM - QPART), f32)
        rest = jnp.zeros((32, 128 - QIM - QPART), f32)
        piece[c] = jnp.concatenate([re, pad, im, rest], axis=1).astype(bf16)
    rel = rel_ref[...]
    owner = jnp.right_shift(rel * 4520, 17)
    index[s] = jnp.concatenate(
        [
            src_ref[...],
            rel + owner * (32 - OWN_RELS),
            dst_ref[...] + s * 256,
            jnp.broadcast_to(count_ref[...], (1, 1024)),
            jnp.zeros((4, 1024), jnp.int32),
        ],
        axis=0,
    )
    low[0] = home_ref[...].astype(bf16)
    low[1] = visit_ref[...].astype(bf16)
    low_all[s] = low[...]
    greeted(peers)
    started = []

    def go(copy):
        copy.start()
        started.append(copy)
        return copy

    def to_span(src_of, dst, send, recv):
        return [
            go(remote(src_of(lax.rem(s + d, 4)), dst, send.at[d - 1], recv.at[d - 1], span_peers[d - 1]))
            for d in (1, 2, 3)
        ]

    pieces = to_span(lambda peer: piece.at[peer], got_piece.at[s], p_send, p_recv)
    lists = to_span(lambda peer: index.at[s], index.at[s], i_send, i_recv)
    got_piece[s] = piece[s]
    for copy in pieces:
        copy.wait_recv()
    block = jnp.concatenate([got_piece[c].astype(f32) for c in range(4)], axis=0).T
    table[yh, z, x] = block[:QROWS].astype(bf16)

    own = table.at[yh, z, x]
    other = table.at[yo, z, x]
    y_copy = go(remote(own, own, y_send, y_recv, y_peer))
    x_copies = [
        go(remote(own, own, x_send.at[d - 1], x_recv.at[d - 1], x_peers[d - 1])) for d in (1, 2, 3)
    ]
    lows = [[], []]
    for k in (0, 1):
        for number, peer in enumerate((across, mate)):
            lows[k].append(
                go(remote(low.at[k], low_all.at[s, k], h_send.at[k, number], h_recv.at[k, number], peer))
            )

    def relay(k):
        lows[k][0].wait_recv()
        ref = low_all.at[across_span, k]
        lows[k].append(go(remote(ref, ref, h_send.at[k, 2], h_recv.at[k, 2], mate)))

    for copy in lists:
        copy.wait_recv()

    at = lax.broadcasted_iota(jnp.int32, (8, LIVE), 1)
    kind = lax.broadcasted_iota(jnp.int32, (8, LIVE), 0)
    slots = jnp.full((8, LIVE), -1, jnp.int32)
    start = jnp.zeros((1, 1), jnp.int32)
    for c in range(4):
        part = index[c]
        end = start + part[3:4, 0:1]
        listed = jnp.concatenate([part, jnp.zeros((8, LIVE - 1024), jnp.int32)], axis=1)
        if c:
            for bit in range(11):
                on = jnp.bitwise_and(jnp.right_shift(start, bit), 1) == 1
                listed = jnp.where(on, pltpu.roll(listed, 1 << bit, 1), listed)
        slots = jnp.where((at >= start) & (at < end), listed, slots)
        start = end
    slots = jnp.where(kind == 3, jnp.where(at < start, 1, 0), slots)
    share_slots = jnp.zeros((8, SHARE), jnp.int32)
    for c in range(4):
        share_slots = jnp.where(s == c, slots[:, c * SHARE : (c + 1) * SHARE], share_slots)
    spot = slots[1:2]
    group = jnp.right_shift(spot, 7)
    low_hot[...] = one_hot(128, jnp.bitwise_and(spot, 127))
    total[...] = jnp.zeros_like(total)

    def half(chunk):
        return yh if chunk == 0 else yo

    def gather(chunk, zz):
        zz = lax.rem(zz + 8, 8)
        hot_lanes(low_hot, hot, group, half(chunk) * 32 + zz * 4)
        block = jnp.concatenate([table[half(chunk), zz, k] for k in range(4)], axis=1)
        total[...] += jnp.dot(block, hot[...], preferred_element_type=f32)

    flying = {}
    turns = {"r": 4, "l": 3}
    rows = {}

    def pass_on(way, step, key, send, recv, ref):
        flying[(key, way, step)] = go(remote(ref, ref, send, recv, right if way == "r" else left))

    def along_x(number, ref):
        rows[number] = [
            go(remote(ref, ref, w_send.at[number, d - 1], w_recv.at[number, d - 1], x_peers[d - 1]))
            for d in (1, 2, 3)
        ]

    def gather_row(number, zz):
        for copy in rows[number]:
            copy.wait_recv()
        gather(1, zz)

    for step in range(5):
        if step == 0:
            y_copy.wait_recv()
            along_x(0, other)
        for way in ("r", "l"):
            zz = z - step if way == "r" else z + step
            ref = table.at[yo, lax.rem(zz + 8, 8), x]
            if 1 <= step <= turns[way]:
                flying[("other", way, step - 1)].wait_recv()
            if step < turns[way]:
                send, recv = (b_send, b_recv) if way == "r" else (c_send, c_recv)
                pass_on(way, step, "other", send.at[step], recv.at[step], ref)
            if 1 <= step <= turns[way]:
                along_x(step if way == "r" else 4 + step, ref)
        if step == 0:
            for copy in x_copies:
                copy.wait_recv()
        for part in (0, 1):
            for way in ("r", "l"):
                if 1 <= step <= FAR[(way, part)]:
                    flying[(part, way, step - 1)].wait_recv()
                if step < FAR[(way, part)]:
                    zz = z - step if way == "r" else z + step
                    ref = table.at[yh, lax.rem(zz + 8, 8), pl.ds(2 * part, 2)]
                    send, recv = (r_send, r_recv) if way == "r" else (l_send, l_recv)
                    pass_on(way, step, part, send.at[part, step], recv.at[part, step], ref)
        if step == 0:
            gather(0, z)
        else:
            gather(0, z - step)
            if step < 4:
                gather(0, z + step)
            if step == 1:
                gather_row(0, z)
            else:
                gather_row(step - 1, z - step + 1)
                gather_row(step + 3, z + step - 1)
        if step in (1, 2):
            relay(step - 1)
    gather_row(4, z - 4)
    for c in range(4):
        mine[c] = total[:, c * SHARE : (c + 1) * SHARE].astype(bf16)
    picks = to_span(lambda peer: mine.at[peer], picked.at[s], k_send, k_recv)
    picked[s] = mine[s]
    moves = [
        go(remote(visit_ref, visit_out, v_send.at[0], v_recv.at[0], after)),
        go(remote(visit_state_ref, visit_state_out, v_send.at[1], v_recv.at[1], after)),
    ]

    for copy in lows[0][1:]:
        copy.wait_recv()
    hot_neg[...] = one_hot(1024, neg_ref[...])
    home = jnp.concatenate([low_all[c, 0] for c in range(4)], axis=1)
    found = jnp.dot(home, hot_neg[...], preferred_element_type=f32)
    negatives[...] = found.astype(bf16)
    negatives_t[...] = found.T.astype(bf16)
    for copy in lows[1][1:]:
        copy.wait_recv()
    visit = jnp.concatenate([low_all[c, 1] for c in range(4)], axis=1)
    live = share_slots[3:4, :].astype(f32)
    hot_source = one_hot(1024, share_slots[0:1, :])
    hot_dest = one_hot(1024, share_slots[2:3, :])
    source = jnp.dot(home, hot_source, preferred_element_type=f32)
    dest = jnp.dot(visit, hot_dest, preferred_element_type=f32)
    dest_re, dest_im = dest[:middle], dest[middle:]
    for copy in picks:
        copy.wait_recv()
    rel = [picked[c].astype(f32) for c in range(4)]
    rel_re = jnp.concatenate([part[:QPART] for part in rel], axis=0)
    rel_im = jnp.concatenate([part[QIM : QIM + QPART] for part in rel], axis=0)
    trans = jnp.concatenate(
        [rel_re * dest_re - rel_im * dest_im, rel_re * dest_im + rel_im * dest_re], axis=0
    ).astype(bf16)
    positive = jnp.sum(source * trans.astype(f32), axis=0, keepdims=True)
    score = jnp.dot(negatives_t[...], trans, preferred_element_type=f32)
    pos_weight = -live * jax.nn.sigmoid(-positive)
    weight = (live * jax.nn.sigmoid(score) * (1.0 / 1024.0)).astype(bf16)
    pull = jnp.dot(negatives[...], weight, preferred_element_type=f32)
    grad = pos_weight * source + pull
    grad_re, grad_im = grad[:middle], grad[middle:]
    out_re = dest_re * grad_re + dest_im * grad_im
    out_im = dest_re * grad_im - dest_im * grad_re
    pad = jnp.zeros((QIM - QPART, SHARE), f32)
    for c in range(4):
        part = slice(c * QPART, (c + 1) * QPART)
        high, rest = halves(jnp.concatenate([out_re[part], pad, out_im[part], pad], axis=0))
        rel_grad[0, c] = high
        rel_grad[1, c] = rest
    swaps = [
        to_span(lambda peer: rel_grad.at[i, peer], rel_got.at[i, s], a_send.at[i], a_recv.at[i]) for i in (0, 1)
    ]
    for i in (0, 1):
        rel_got[i, s] = rel_grad[i, s]
    grad_dest = jnp.concatenate(
        [rel_re * grad_re + rel_im * grad_im, rel_re * grad_im - rel_im * grad_re], axis=0
    )
    dest_high, dest_low = halves(grad_dest)
    visit_grad = lax.dot_general(dest_high, hot_dest, NT, preferred_element_type=f32) + lax.dot_general(
        dest_low, hot_dest, NT, preferred_element_type=f32
    )
    share = jnp.dot(hot_neg[...], weight, preferred_element_type=f32) + pos_weight * hot_source.astype(f32)
    share_high, share_low = halves(share)
    home_grad = lax.dot_general(trans, share_high, NT, preferred_element_type=f32) + lax.dot_general(
        trans, share_low, NT, preferred_element_type=f32
    )
    for c in range(4):
        grads[c, 0] = home_grad[:, c * 256 : (c + 1) * 256]
        grads[c, 1] = visit_grad[:, c * 256 : (c + 1) * 256]

    def take(i):
        for copy in swaps[i]:
            copy.wait_recv()
        for c in range(4):
            both[i * QROWS : (i + 1) * QROWS, c * SHARE : (c + 1) * SHARE] = rel_got[i, c]

    def scatter(chunk, zz, fine=True):
        hot_lanes(low_hot, hot, group, half(chunk) * 32 + lax.rem(zz + 8, 8) * 4)
        if fine:
            sums = lax.dot_general(both[...], hot[...], NT, preferred_element_type=f32)
            sums = sums[:QROWS] + sums[QROWS:]
        else:
            sums = lax.dot_general(both[:QROWS], hot[...], NT, preferred_element_type=f32)
        return [sums[:, k * 128 : (k + 1) * 128] for k in range(4)]

    back = {}

    def ring(dist):
        value = None
        for way in ("r", "l"):
            zz = z + dist if way == "r" else z - dist
            buf, got, send, recv = (
                (r_buf, r_got, rr_send, rr_recv) if way == "r" else (l_buf, l_got, ll_send, ll_recv)
            )
            if dist < 4 or value is None:
                value = scatter(0, zz, dist < 4)
            for part in (0, 1):
                if dist > FAR[(way, part)]:
                    continue
                if dist < FAR[(way, part)]:
                    back[(part, way, dist + 1)].wait_recv()
                for k in (0, 1):
                    here = value[2 * part + k]
                    if dist < FAR[(way, part)]:
                        here = here + got[part, dist, k].astype(f32)
                    buf[part, dist - 1, k] = here.astype(bf16)
                back[(part, way, dist)] = go(
                    remote(
                        buf.at[part, dist - 1], got.at[part, dist - 1],
                        send.at[part, dist - 1], recv.at[part, dist - 1],
                        right if way == "r" else left,
                    )
                )

    x_rows = {}

    def sow(number, zz, fine=True):
        value = scatter(1, zz, fine)
        for k in range(4):
            kept[number, k] = value[k]
            cast[number, k] = value[k].astype(bf16)
        x_rows[number] = [
            go(
                remote(
                    cast.at[number, lax.rem(x + d, 4)], x_in.at[number, d - 1],
                    xb_send.at[number, d - 1], xb_recv.at[number, d - 1], x_peers[d - 1],
                )
            )
            for d in (1, 2, 3)
        ]

    def reap(number):
        for copy in x_rows[number]:
            copy.wait_recv()
        return kept[number, x] + sum(x_in[number, d].astype(f32) for d in range(3))

    def ring_row(dist):
        for i, way in enumerate(("r", "l")):
            if dist > turns[way]:
                continue
            value = reap(dist if way == "r" else 4 + dist)
            if dist < turns[way]:
                back[("other", way, dist + 1)].wait_recv()
                value = value + one_got[i, dist]
            one_buf[i, dist - 1] = value
            back[("other", way, dist)] = go(
                remote(
                    one_buf.at[i, dist - 1], one_got.at[i, dist - 1],
                    e_send.at[i, dist - 1], e_recv.at[i, dist - 1], right if way == "r" else left,
                )
            )

    m_copies = {}
    o_copies = {}

    def to_mate(k):
        for i, row in ((1, across_mate), (0, mate_span)):
            m_copies[(i, k)] = go(remote(grads.at[row, k], m_got.at[i, k], m_send.at[i, k], m_recv.at[i, k], mate))

    def cross(k):
        m_copies[(1, k)].wait_recv()
        o_buf[k] = (grads[across_span, k] + m_got[1, k]).astype(bf16)
        o_copies[k] = go(remote(o_buf.at[k], o_got.at[k], o_send.at[k], o_recv.at[k], across))

    def summed(k):
        m_copies[(0, k)].wait_recv()
        o_copies[k].wait_recv()
        return grads[s, k] + m_got[0, k] + o_got[k].astype(f32)

    take(0)
    sow(4, z + 4, False)
    ring(4)
    to_mate(1)
    take(1)
    sow(3, z + 3)
    sow(7, z - 3)
    ring(3)
    ring_row(4)
    to_mate(0)
    sow(2, z + 2)
    sow(6, z - 2)
    ring(2)
    ring_row(3)
    cross(1)
    sow(1, z + 1)
    sow(5, z - 1)
    ring(1)
    ring_row(2)
    cross(0)
    visit_sum[...] = summed(1).astype(bf16)
    moves.append(go(remote(visit_sum, visit_grad_ref, v_send.at[2], v_recv.at[2], after)))
    sow(0, z)
    ring_row(1)
    near = scatter(0, z)
    for part in (0, 1):
        back[(part, "r", 1)].wait_recv()
        back[(part, "l", 1)].wait_recv()
        for k in (0, 1):
            row_sum[2 * part + k] = (
                near[2 * part + k] + r_got[part, 0, k].astype(f32) + l_got[part, 0, k].astype(f32)
            )
    x_copies = [
        go(
            remote(
                row_sum.at[lax.rem(x + d, 4)], x_got.at[d - 1],
                xx_send.at[d - 1], xx_recv.at[d - 1], x_peers[d - 1],
            )
        )
        for d in (1, 2, 3)
    ]
    for way in ("r", "l"):
        back[("other", way, 1)].wait_recv()
    x_sum[...] = reap(0) + one_got[0, 0] + one_got[1, 0]
    y_copy = go(remote(x_sum, y_got, yy_send, yy_recv, y_peer))
    home_grad_ref[...] = summed(0)
    for copy in x_copies:
        copy.wait_recv()
    here = row_sum[x] + x_got[0] + x_got[1] + x_got[2]
    y_copy.wait_recv()
    turned = jnp.concatenate([here + y_got[...], jnp.zeros((128 - QROWS, 128), f32)], axis=0).T
    for c in range(4):
        q_buf[c] = turned[32 * c : 32 * (c + 1)]
    quarter_ref[s] = q_buf[s]
    for copy in to_span(lambda peer: q_buf.at[peer], quarter_ref.at[s], q_send, q_recv) + moves:
        copy.wait_recv()
    for copy in started:
        copy.wait_send()


def bucket_round(src, rel, dst, count, neg_rows, home, visit, visit_state, relation):
    dma = pltpu.SemaphoreType.DMA
    bf16, f32, i32 = jnp.bfloat16, jnp.float32, jnp.int32
    pair = (2,) + home.shape
    quarters = (4, QROWS, SHARE)
    ring = pltpu.VMEM((2, 4, 2, QROWS, 128), bf16)
    lone = pltpu.VMEM((2, 4, QROWS, 128), f32)
    rows = home.shape[0]
    return pl.pallas_call(
        round_kernel,
        out_shape=(
            jax.ShapeDtypeStruct(home.shape, f32),
            jax.ShapeDtypeStruct(visit.shape, f32),
            jax.ShapeDtypeStruct(visit_state.shape, f32),
            jax.ShapeDtypeStruct(visit.shape, bf16),
            jax.ShapeDtypeStruct((4, 32, 128), f32),
        ),
        in_specs=[VMEM] * 9,
        out_specs=(VMEM,) * 5,
        scratch_shapes=[
            pltpu.VMEM(pair, bf16), pltpu.VMEM((4,) + pair, bf16),
            pltpu.VMEM((4, 32, 128), bf16), pltpu.VMEM((4, 32, 128), bf16),
            pltpu.VMEM((4, 8, 1024), i32), pltpu.VMEM((2, 8, 4, QROWS, 128), bf16),
            pltpu.VMEM((128, LIVE), bf16), pltpu.VMEM((512, LIVE), bf16), pltpu.VMEM((QROWS, LIVE), f32),
            pltpu.VMEM(quarters, bf16), pltpu.VMEM(quarters, bf16),
            pltpu.VMEM((1024, 1024), bf16), pltpu.VMEM((rows, 1024), bf16),
            pltpu.VMEM((2,) + quarters, bf16), pltpu.VMEM((2,) + quarters, bf16), pltpu.VMEM((2 * QROWS, LIVE), bf16),
            pltpu.VMEM((4,) + pair, f32),
            ring, ring, ring, ring,
            pltpu.VMEM((4, QROWS, 128), f32), pltpu.VMEM((3, QROWS, 128), f32),
            pltpu.VMEM((QROWS, 128), f32), pltpu.VMEM((QROWS, 128), f32), pltpu.VMEM((4, 32, 128), f32),
            pltpu.VMEM((2,) + pair, f32), pltpu.VMEM(pair, bf16), pltpu.VMEM(pair, bf16),
            pltpu.VMEM(visit.shape, bf16),
            pltpu.VMEM((1024, rows), bf16), pltpu.VMEM((8, 4, QROWS, 128), f32), pltpu.VMEM((8, 4, QROWS, 128), bf16),
            pltpu.VMEM((8, 3, QROWS, 128), bf16), lone, lone,
            dma((3,)), dma((3,)), dma((3,)), dma((3,)), dma((2, 3)), dma((2, 3)), dma, dma,
            dma((3,)), dma((3,)), dma((2, 4)), dma((2, 4)), dma((2, 4)), dma((2, 4)),
            dma((3,)), dma((3,)), dma((3,)), dma((3,)), dma((2, 3)), dma((2, 3)),
            dma((2, 4)), dma((2, 4)), dma((2, 4)), dma((2, 4)), dma((3,)), dma((3,)),
            dma, dma, dma((3,)), dma((3,)), dma((2, 2)), dma((2, 2)), dma((2,)), dma((2,)),
            dma((4,)), dma((4,)), dma((4,)), dma((4,)), dma((8, 3)), dma((8, 3)),
            dma((8, 3)), dma((8, 3)), dma((2, 4)), dma((2, 4)),
        ],
        compiler_params=params(0),
        name="bucket_round",
    )(src, rel, dst, count, neg_rows, home, visit, visit_state, relation)


def adagrad(table, state, grad_in, axis):
    state_new = state + jnp.sum(grad_in * grad_in, axis=axis, keepdims=True) * (1.0 / grad_in.shape[axis])
    return table - LEARN_RATE * grad_in / (jnp.sqrt(state_new) + ADAGRAD_EPS), state_new


def update_kernel(
    home_grad_ref, home_ref, home_state_ref, visit_grad_ref, visit_ref, visit_state_ref,
    quarter_ref, relation_ref, relation_state_ref,
    home_out, home_state_out, visit_out, visit_state_out, relation_out, relation_state_out,
):
    f32 = jnp.float32
    home_out[...], home_state_out[...] = adagrad(home_ref[...], home_state_ref[...], home_grad_ref[...], 0)
    visit_out[...], visit_state_out[...] = adagrad(
        visit_ref[...], visit_state_ref[...], visit_grad_ref[...].astype(f32), 0
    )
    grad = jnp.concatenate(
        [quarter_ref[c][:, first : first + QPART] for first in (0, QIM) for c in range(4)], axis=1
    )[:OWN_RELS]
    diagonal = lax.broadcasted_iota(jnp.int32, (OWN_RELS, OWN_RELS), 0) == lax.broadcasted_iota(
        jnp.int32, (OWN_RELS, OWN_RELS), 1
    )
    state = jnp.sum(jnp.where(diagonal, relation_state_ref[...], 0.0), axis=1, keepdims=True)
    relation_out[...], state = adagrad(relation_ref[...], state, grad, 1)
    relation_state_out[...] = jnp.sum(jnp.where(diagonal, state, 0.0), axis=0, keepdims=True)


def update(*arrays):
    shape = lambda a: jax.ShapeDtypeStruct(a.shape, jnp.float32)
    return pl.pallas_call(
        update_kernel,
        out_shape=tuple(shape(arrays[i]) for i in (1, 2, 4, 5, 7, 8)),
        in_specs=[VMEM] * 9,
        out_specs=(VMEM,) * 6,
        compiler_params=params(),
        name="update",
    )(*arrays)


def shards(
    home_table, home_state, visit_table, visit_state, relation_table, relation_state,
    edge_src, edge_rel, edge_dst, edge_count, neg_rows,
):
    home_grad, moved, moved_state, moved_grad, quarters = bucket_round(
        edge_src[0], edge_rel[0], edge_dst[0], edge_count, neg_rows,
        home_table, visit_table, visit_state[None], relation_table.T,
    )
    new_home, new_home_state, new_visit, new_visit_state, new_relation, new_relation_state = update(
        home_grad, home_table, home_state[None], moved_grad, moved, moved_state,
        quarters, relation_table.T, relation_state[None],
    )
    return (new_home, new_home_state[0], new_visit, new_visit_state[0], new_relation.T, new_relation_state[0])


def solution(mesh):
    cols = P(None, ("blk", "span"))
    rows = P(("blk", "span"))
    slot = P("blk", "span", None)
    return jax.shard_map(
        shards,
        mesh=mesh,
        in_specs=(cols, rows, cols, rows, cols, rows, slot, slot, slot, P("blk", "span"), P("blk", None)),
        out_specs=(cols, rows, cols, rows, cols, rows),
        check_vma=False,
    )
```

```python
import functools

import jax
import jax.numpy as jnp
from jax import lax
from jax.experimental import pallas as pl
from jax.experimental.pallas import tpu as pltpu
from jax.sharding import PartitionSpec as P

LEARN_RATE = 0.1
ADAGRAD_EPS = 1e-10
MESH = pl.DeviceIdType.MESH
LIVE = 1536
SHARE = 384
QROWS = 112
QPART = 50
QIM = 56
OWN_RELS = 29
VMEM = pl.BlockSpec(memory_space=pltpu.VMEM)
SMEM = pl.BlockSpec(memory_space=pltpu.SMEM)
NT = (((1,), (1,)), ((), ()))


def params(collective_id=None):
    if collective_id is None:
        return pltpu.CompilerParams(vmem_limit_bytes=56 * 2**20)
    return pltpu.CompilerParams(
        vmem_limit_bytes=56 * 2**20, collective_id=collective_id, has_side_effects=True
    )


def place():
    blk = lax.axis_index("blk")
    span = lax.axis_index("span")
    yh = lax.div(blk, 32)
    z = lax.rem(lax.div(blk, 4), 8)
    x = lax.rem(blk, 4)
    return yh, z, x, span


def device(yh, z, x, span):
    return (yh * 32 + lax.rem(z + 8, 8) * 4 + lax.rem(x + 4, 4), lax.rem(span, 4))


def remote(src, dst, send, recv, where):
    return pltpu.make_async_remote_copy(
        src_ref=src, dst_ref=dst, send_sem=send, recv_sem=recv, device_id=where, device_id_type=MESH
    )


def greet(peers):
    barrier = pltpu.get_barrier_semaphore()
    for peer in peers:
        pl.semaphore_signal(barrier, inc=1, device_id=peer, device_id_type=MESH)


def greeted(peers):
    pl.semaphore_wait(pltpu.get_barrier_semaphore(), len(peers))


def one_hot(rows, index):
    row = lax.broadcasted_iota(jnp.int32, (rows, index.shape[1]), 0)
    return jnp.where(row == index, 1.0, 0.0).astype(jnp.bfloat16)


def halves(value):
    high = value.astype(jnp.bfloat16)
    return high, (value - high.astype(jnp.float32)).astype(jnp.bfloat16)


def hot_lanes(low_hot, hot, group, first):
    for k in range(4):
        mask = jnp.where(group == first + k, 1.0, 0.0).astype(jnp.bfloat16)
        hot[k * 128 : (k + 1) * 128, :] = low_hot[...] * mask


FAR = {("r", 0): 4, ("r", 1): 3, ("l", 0): 3, ("l", 1): 4}


def round_kernel(
    src_ref, rel_ref, dst_ref, count_ref, neg_ref, home_ref, visit_ref, visit_state_ref, relation_ref,
    home_grad_ref, visit_out, visit_state_out, quarter_ref,
    low, low_all, piece, got_piece, index, table, low_hot, hot, total, mine, picked,
    hot_neg, negatives, rel_grad, rel_got, both, grads,
    r_buf, r_got, l_buf, l_got, row_sum, x_got, x_sum, y_got, q_buf, m_got, o_buf, o_got, moved, moved_state,
    negatives_t, kept, cast, x_in, one_buf, one_got,
    i_send, i_recv, p_send, p_recv, h_send, h_recv, y_send, y_recv, x_send, x_recv,
    r_send, r_recv, l_send, l_recv, k_send, k_recv, v_send, v_recv, a_send, a_recv,
    rr_send, rr_recv, ll_send, ll_recv, xx_send, xx_recv, yy_send, yy_recv, q_send, q_recv,
    m_send, m_recv, o_send, o_recv, b_send, b_recv, c_send, c_recv, w_send, w_recv,
    xb_send, xb_recv, e_send, e_recv,
):
    f32, bf16 = jnp.float32, jnp.bfloat16
    yh, z, x, s = place()
    yo = 1 - yh
    blk = lax.axis_index("blk")
    span_peers = [device(yh, z, x, s + d) for d in (1, 2, 3)]
    x_peers = [device(yh, z, x + d, s) for d in (1, 2, 3)]
    y_peer = device(yo, z, x, s)
    right = device(yh, z + 1, x, s)
    left = device(yh, z - 1, x, s)
    after = (lax.rem(blk + 1, 64), s)
    before = (lax.rem(blk + 63, 64), s)
    mate_span = lax.div(s, 2) * 2 + 1 - lax.rem(s, 2)
    mate = device(yh, z, x, mate_span)
    across_span = lax.rem(s + 2, 4)
    across = device(yh, z, x, across_span)
    across_mate = lax.rem(mate_span + 2, 4)
    peers = span_peers + x_peers + [y_peer, right, left, after, before]
    greet(peers)

    middle = 4 * QPART
    spare = jnp.zeros((32 - OWN_RELS, 2 * middle), f32)
    operators = jnp.concatenate([relation_ref[...], spare], axis=0)
    for c in range(4):
        re = operators[:, c * QPART : (c + 1) * QPART]
        im = operators[:, middle + c * QPART : middle + (c + 1) * QPART]
        pad = jnp.zeros((32, QIM - QPART), f32)
        rest = jnp.zeros((32, 128 - QIM - QPART), f32)
        piece[c] = jnp.concatenate([re, pad, im, rest], axis=1).astype(bf16)
    greeted(peers)
    started = []

    def go(copy):
        copy.start()
        started.append(copy)
        return copy

    def to_span(src_of, dst, send, recv):
        return [
            go(remote(src_of(lax.rem(s + d, 4)), dst, send.at[d - 1], recv.at[d - 1], span_peers[d - 1]))
            for d in (1, 2, 3)
        ]

    pieces = to_span(lambda peer: piece.at[peer], got_piece.at[s], p_send, p_recv)
    rel = rel_ref[...]
    owner = jnp.right_shift(rel * 4520, 17)
    index[s] = jnp.concatenate(
        [
            src_ref[...],
            rel + owner * (32 - OWN_RELS),
            dst_ref[...] + s * 256,
            jnp.broadcast_to(count_ref[...], (1, 1024)),
            jnp.zeros((4, 1024), jnp.int32),
        ],
        axis=0,
    )
    lists = to_span(lambda peer: index.at[s], index.at[s], i_send, i_recv)
    got_piece[s] = piece[s]
    for copy in pieces:
        copy.wait_recv()
    block = jnp.concatenate([got_piece[c].astype(f32) for c in range(4)], axis=0).T
    table[yh, z, x] = block[:QROWS].astype(bf16)

    own = table.at[yh, z, x]
    other = table.at[yo, z, x]
    y_copy = go(remote(own, own, y_send, y_recv, y_peer))
    x_copies = [
        go(remote(own, own, x_send.at[d - 1], x_recv.at[d - 1], x_peers[d - 1])) for d in (1, 2, 3)
    ]
    low[0] = home_ref[...].astype(bf16)
    low[1] = visit_ref[...].astype(bf16)
    low_all[s] = low[...]
    lows = [[], []]
    for k in (0, 1):
        for number, peer in enumerate((across, mate)):
            lows[k].append(
                go(remote(low.at[k], low_all.at[s, k], h_send.at[k, number], h_recv.at[k, number], peer))
            )

    def relay(k):
        lows[k][0].wait_recv()
        ref = low_all.at[across_span, k]
        lows[k].append(go(remote(ref, ref, h_send.at[k, 2], h_recv.at[k, 2], mate)))

    for copy in lists:
        copy.wait_recv()

    at = lax.broadcasted_iota(jnp.int32, (8, LIVE), 1)
    kind = lax.broadcasted_iota(jnp.int32, (8, LIVE), 0)
    slots = jnp.full((8, LIVE), -1, jnp.int32)
    start = jnp.zeros((1, 1), jnp.int32)
    for c in range(4):
        part = index[c]
        end = start + part[3:4, 0:1]
        listed = jnp.concatenate([part, jnp.zeros((8, LIVE - 1024), jnp.int32)], axis=1)
        if c:
            for bit in range(11):
                on = jnp.bitwise_and(jnp.right_shift(start, bit), 1) == 1
                listed = jnp.where(on, pltpu.roll(listed, 1 << bit, 1), listed)
        slots = jnp.where((at >= start) & (at < end), listed, slots)
        start = end
    slots = jnp.where(kind == 3, jnp.where(at < start, 1, 0), slots)
    share_slots = jnp.zeros((8, SHARE), jnp.int32)
    for c in range(4):
        share_slots = jnp.where(s == c, slots[:, c * SHARE : (c + 1) * SHARE], share_slots)
    spot = slots[1:2]
    group = jnp.right_shift(spot, 7)
    low_hot[...] = one_hot(128, jnp.bitwise_and(spot, 127))
    total[...] = jnp.zeros_like(total)

    def half(chunk):
        return yh if chunk == 0 else yo

    def gather(chunk, zz):
        zz = lax.rem(zz + 8, 8)
        hot_lanes(low_hot, hot, group, half(chunk) * 32 + zz * 4)
        block = jnp.concatenate([table[half(chunk), zz, k] for k in range(4)], axis=1)
        total[...] += jnp.dot(block, hot[...], preferred_element_type=f32)

    flying = {}
    turns = {"r": 4, "l": 3}
    rows = {}

    def pass_on(way, step, key, send, recv, ref):
        flying[(key, way, step)] = go(remote(ref, ref, send, recv, right if way == "r" else left))

    def along_x(number, ref):
        rows[number] = [
            go(remote(ref, ref, w_send.at[number, d - 1], w_recv.at[number, d - 1], x_peers[d - 1]))
            for d in (1, 2, 3)
        ]

    def gather_row(number, zz):
        for copy in rows[number]:
            copy.wait_recv()
        gather(1, zz)

    for step in range(5):
        if step == 0:
            y_copy.wait_recv()
            along_x(0, other)
        for way in ("r", "l"):
            zz = z - step if way == "r" else z + step
            ref = table.at[yo, lax.rem(zz + 8, 8), x]
            if 1 <= step <= turns[way]:
                flying[("other", way, step - 1)].wait_recv()
            if step < turns[way]:
                send, recv = (b_send, b_recv) if way == "r" else (c_send, c_recv)
                pass_on(way, step, "other", send.at[step], recv.at[step], ref)
            if 1 <= step <= turns[way]:
                along_x(step if way == "r" else 4 + step, ref)
        if step == 0:
            for copy in x_copies:
                copy.wait_recv()
        for part in (0, 1):
            for way in ("r", "l"):
                if 1 <= step <= FAR[(way, part)]:
                    flying[(part, way, step - 1)].wait_recv()
                if step < FAR[(way, part)]:
                    zz = z - step if way == "r" else z + step
                    ref = table.at[yh, lax.rem(zz + 8, 8), pl.ds(2 * part, 2)]
                    send, recv = (r_send, r_recv) if way == "r" else (l_send, l_recv)
                    pass_on(way, step, part, send.at[part, step], recv.at[part, step], ref)
        if step == 0:
            gather(0, z)
        else:
            gather(0, z - step)
            if step < 4:
                gather(0, z + step)
            if step == 1:
                gather_row(0, z)
            else:
                gather_row(step - 1, z - step + 1)
                gather_row(step + 3, z + step - 1)
        if step in (1, 2):
            relay(step - 1)
    gather_row(4, z - 4)
    for c in range(4):
        mine[c] = total[:, c * SHARE : (c + 1) * SHARE].astype(bf16)
    picks = to_span(lambda peer: mine.at[peer], picked.at[s], k_send, k_recv)
    picked[s] = mine[s]

    for copy in lows[0][1:]:
        copy.wait_recv()
    hot_neg[...] = one_hot(1024, neg_ref[...])
    home = jnp.concatenate([low_all[c, 0] for c in range(4)], axis=1)
    found = jnp.dot(home, hot_neg[...], preferred_element_type=f32)
    negatives[...] = found.astype(bf16)
    negatives_t[...] = found.T.astype(bf16)
    for copy in lows[1][1:]:
        copy.wait_recv()
    visit = jnp.concatenate([low_all[c, 1] for c in range(4)], axis=1)
    live = share_slots[3:4, :].astype(f32)
    hot_source = one_hot(1024, share_slots[0:1, :])
    hot_dest = one_hot(1024, share_slots[2:3, :])
    source = jnp.dot(home, hot_source, preferred_element_type=f32)
    dest = jnp.dot(visit, hot_dest, preferred_element_type=f32)
    dest_re, dest_im = dest[:middle], dest[middle:]
    for copy in picks:
        copy.wait_recv()
    rel = [picked[c].astype(f32) for c in range(4)]
    rel_re = jnp.concatenate([part[:QPART] for part in rel], axis=0)
    rel_im = jnp.concatenate([part[QIM : QIM + QPART] for part in rel], axis=0)
    trans = jnp.concatenate(
        [rel_re * dest_re - rel_im * dest_im, rel_re * dest_im + rel_im * dest_re], axis=0
    ).astype(bf16)
    positive = jnp.sum(source * trans.astype(f32), axis=0, keepdims=True)
    score = jnp.dot(negatives_t[...], trans, preferred_element_type=f32)
    pos_weight = -live * jax.nn.sigmoid(-positive)
    weight = (live * jax.nn.sigmoid(score) * (1.0 / 1024.0)).astype(bf16)
    pull = jnp.dot(negatives[...], weight, preferred_element_type=f32)
    grad = pos_weight * source + pull
    grad_re, grad_im = grad[:middle], grad[middle:]
    out_re = dest_re * grad_re + dest_im * grad_im
    out_im = dest_re * grad_im - dest_im * grad_re
    pad = jnp.zeros((QIM - QPART, SHARE), f32)
    for c in range(4):
        part = slice(c * QPART, (c + 1) * QPART)
        high, rest = halves(jnp.concatenate([out_re[part], pad, out_im[part], pad], axis=0))
        rel_grad[0, c] = high
        rel_grad[1, c] = rest
    swaps = [
        to_span(lambda peer: rel_grad.at[i, peer], rel_got.at[i, s], a_send.at[i], a_recv.at[i]) for i in (0, 1)
    ]
    for i in (0, 1):
        rel_got[i, s] = rel_grad[i, s]
    grad_dest = jnp.concatenate(
        [rel_re * grad_re + rel_im * grad_im, rel_re * grad_im - rel_im * grad_re], axis=0
    )
    dest_high, dest_low = halves(grad_dest)
    visit_grad = lax.dot_general(dest_high, hot_dest, NT, preferred_element_type=f32) + lax.dot_general(
        dest_low, hot_dest, NT, preferred_element_type=f32
    )
    m_copies = {}

    def to_mate(k):
        for i, row in ((1, across_mate), (0, mate_span)):
            m_copies[(i, k)] = go(remote(grads.at[row, k], m_got.at[i, k], m_send.at[i, k], m_recv.at[i, k], mate))

    for c in range(4):
        grads[c, 1] = visit_grad[:, c * 256 : (c + 1) * 256]
    to_mate(1)
    share = jnp.dot(hot_neg[...], weight, preferred_element_type=f32) + pos_weight * hot_source.astype(f32)
    share_high, share_low = halves(share)
    home_grad = lax.dot_general(trans, share_high, NT, preferred_element_type=f32) + lax.dot_general(
        trans, share_low, NT, preferred_element_type=f32
    )
    for c in range(4):
        grads[c, 0] = home_grad[:, c * 256 : (c + 1) * 256]
    to_mate(0)

    def take(i):
        for copy in swaps[i]:
            copy.wait_recv()
        for c in range(4):
            both[i * QROWS : (i + 1) * QROWS, c * SHARE : (c + 1) * SHARE] = rel_got[i, c]

    def scatter(chunk, zz, fine=True):
        hot_lanes(low_hot, hot, group, half(chunk) * 32 + lax.rem(zz + 8, 8) * 4)
        if fine:
            sums = lax.dot_general(both[...], hot[...], NT, preferred_element_type=f32)
            sums = sums[:QROWS] + sums[QROWS:]
        else:
            sums = lax.dot_general(both[:QROWS], hot[...], NT, preferred_element_type=f32)
        return [sums[:, k * 128 : (k + 1) * 128] for k in range(4)]

    back = {}

    def ring(dist):
        value = None
        for way in ("r", "l"):
            zz = z + dist if way == "r" else z - dist
            buf, got, send, recv = (
                (r_buf, r_got, rr_send, rr_recv) if way == "r" else (l_buf, l_got, ll_send, ll_recv)
            )
            if dist < 4 or value is None:
                value = scatter(0, zz, dist < 3)
            for part in (0, 1):
                if dist > FAR[(way, part)]:
                    continue
                if dist < FAR[(way, part)]:
                    back[(part, way, dist + 1)].wait_recv()
                for k in (0, 1):
                    here = value[2 * part + k]
                    if dist < FAR[(way, part)]:
                        here = here + got[part, dist, k].astype(f32)
                    buf[part, dist - 1, k] = here.astype(bf16)
                back[(part, way, dist)] = go(
                    remote(
                        buf.at[part, dist - 1], got.at[part, dist - 1],
                        send.at[part, dist - 1], recv.at[part, dist - 1],
                        right if way == "r" else left,
                    )
                )

    x_rows = {}

    def sow(number, zz, fine=True):
        value = scatter(1, zz, fine)
        for k in range(4):
            kept[number, k] = value[k]
            cast[number, k] = value[k].astype(bf16)
        x_rows[number] = [
            go(
                remote(
                    cast.at[number, lax.rem(x + d, 4)], x_in.at[number, d - 1],
                    xb_send.at[number, d - 1], xb_recv.at[number, d - 1], x_peers[d - 1],
                )
            )
            for d in (1, 2, 3)
        ]

    def reap(number):
        for copy in x_rows[number]:
            copy.wait_recv()
        return kept[number, x] + sum(x_in[number, d].astype(f32) for d in range(3))

    def ring_row(dist):
        for i, way in enumerate(("r", "l")):
            if dist > turns[way]:
                continue
            value = reap(dist if way == "r" else 4 + dist)
            if dist < turns[way]:
                back[("other", way, dist + 1)].wait_recv()
                value = value + one_got[i, dist]
            one_buf[i, dist - 1] = value
            back[("other", way, dist)] = go(
                remote(
                    one_buf.at[i, dist - 1], one_got.at[i, dist - 1],
                    e_send.at[i, dist - 1], e_recv.at[i, dist - 1], right if way == "r" else left,
                )
            )

    o_copies = {}

    def cross(k):
        m_copies[(1, k)].wait_recv()
        o_buf[k] = (grads[across_span, k] + m_got[1, k]).astype(bf16)
        o_copies[k] = go(remote(o_buf.at[k], o_got.at[k], o_send.at[k], o_recv.at[k], across))

    def summed(k):
        m_copies[(0, k)].wait_recv()
        o_copies[k].wait_recv()
        return grads[s, k] + m_got[0, k] + o_got[k].astype(f32)

    take(0)
    sow(4, z + 4, False)
    ring(4)
    cross(1)
    sow(3, z + 3, False)
    sow(7, z - 3, False)
    ring(3)
    ring_row(4)
    take(1)
    cross(0)
    sow(2, z + 2)
    sow(6, z - 2)
    ring(2)
    ring_row(3)
    sow(1, z + 1)
    sow(5, z - 1)
    ring(1)
    ring_row(2)
    moved[...], moved_state[...] = adagrad(visit_ref[...], visit_state_ref[...], summed(1), 0)
    sow(0, z)
    ring_row(1)
    near = scatter(0, z)
    for part in (0, 1):
        back[(part, "r", 1)].wait_recv()
        back[(part, "l", 1)].wait_recv()
        for k in (0, 1):
            row_sum[2 * part + k] = (
                near[2 * part + k] + r_got[part, 0, k].astype(f32) + l_got[part, 0, k].astype(f32)
            )
    x_copies = [
        go(
            remote(
                row_sum.at[lax.rem(x + d, 4)], x_got.at[d - 1],
                xx_send.at[d - 1], xx_recv.at[d - 1], x_peers[d - 1],
            )
        )
        for d in (1, 2, 3)
    ]
    moves = [
        go(remote(moved, visit_out, v_send.at[0], v_recv.at[0], after)),
        go(remote(moved_state, visit_state_out, v_send.at[1], v_recv.at[1], after)),
    ]
    for way in ("r", "l"):
        back[("other", way, 1)].wait_recv()
    x_sum[...] = reap(0) + one_got[0, 0] + one_got[1, 0]
    y_copy = go(remote(x_sum, y_got, yy_send, yy_recv, y_peer))
    home_grad_ref[...] = summed(0)
    for copy in x_copies:
        copy.wait_recv()
    here = row_sum[x] + x_got[0] + x_got[1] + x_got[2]
    y_copy.wait_recv()
    turned = jnp.concatenate([here + y_got[...], jnp.zeros((128 - QROWS, 128), f32)], axis=0).T
    for c in range(4):
        q_buf[c] = turned[32 * c : 32 * (c + 1)]
    quarter_ref[s] = q_buf[s]
    for copy in to_span(lambda peer: q_buf.at[peer], quarter_ref.at[s], q_send, q_recv) + moves:
        copy.wait_recv()
    for copy in started:
        copy.wait_send()


def bucket_round(src, rel, dst, count, neg_rows, home, visit, visit_state, relation):
    dma = pltpu.SemaphoreType.DMA
    bf16, f32, i32 = jnp.bfloat16, jnp.float32, jnp.int32
    pair = (2,) + home.shape
    quarters = (4, QROWS, SHARE)
    ring = pltpu.VMEM((2, 4, 2, QROWS, 128), bf16)
    lone = pltpu.VMEM((2, 4, QROWS, 128), f32)
    rows = home.shape[0]
    return pl.pallas_call(
        round_kernel,
        out_shape=(
            jax.ShapeDtypeStruct(home.shape, f32),
            jax.ShapeDtypeStruct(visit.shape, f32),
            jax.ShapeDtypeStruct(visit_state.shape, f32),
            jax.ShapeDtypeStruct((4, 32, 128), f32),
        ),
        in_specs=[VMEM] * 9,
        out_specs=(VMEM,) * 4,
        scratch_shapes=[
            pltpu.VMEM(pair, bf16), pltpu.VMEM((4,) + pair, bf16),
            pltpu.VMEM((4, 32, 128), bf16), pltpu.VMEM((4, 32, 128), bf16),
            pltpu.VMEM((4, 8, 1024), i32), pltpu.VMEM((2, 8, 4, QROWS, 128), bf16),
            pltpu.VMEM((128, LIVE), bf16), pltpu.VMEM((512, LIVE), bf16), pltpu.VMEM((QROWS, LIVE), f32),
            pltpu.VMEM(quarters, bf16), pltpu.VMEM(quarters, bf16),
            pltpu.VMEM((1024, 1024), bf16), pltpu.VMEM((rows, 1024), bf16),
            pltpu.VMEM((2,) + quarters, bf16), pltpu.VMEM((2,) + quarters, bf16), pltpu.VMEM((2 * QROWS, LIVE), bf16),
            pltpu.VMEM((4,) + pair, f32),
            ring, ring, ring, ring,
            pltpu.VMEM((4, QROWS, 128), f32), pltpu.VMEM((3, QROWS, 128), f32),
            pltpu.VMEM((QROWS, 128), f32), pltpu.VMEM((QROWS, 128), f32), pltpu.VMEM((4, 32, 128), f32),
            pltpu.VMEM((2,) + pair, f32), pltpu.VMEM(pair, bf16), pltpu.VMEM(pair, bf16),
            pltpu.VMEM(visit.shape, f32), pltpu.VMEM(visit_state.shape, f32),
            pltpu.VMEM((1024, rows), bf16), pltpu.VMEM((8, 4, QROWS, 128), f32), pltpu.VMEM((8, 4, QROWS, 128), bf16),
            pltpu.VMEM((8, 3, QROWS, 128), bf16), lone, lone,
            dma((3,)), dma((3,)), dma((3,)), dma((3,)), dma((2, 3)), dma((2, 3)), dma, dma,
            dma((3,)), dma((3,)), dma((2, 4)), dma((2, 4)), dma((2, 4)), dma((2, 4)),
            dma((3,)), dma((3,)), dma((3,)), dma((3,)), dma((2, 3)), dma((2, 3)),
            dma((2, 4)), dma((2, 4)), dma((2, 4)), dma((2, 4)), dma((3,)), dma((3,)),
            dma, dma, dma((3,)), dma((3,)), dma((2, 2)), dma((2, 2)), dma((2,)), dma((2,)),
            dma((4,)), dma((4,)), dma((4,)), dma((4,)), dma((8, 3)), dma((8, 3)),
            dma((8, 3)), dma((8, 3)), dma((2, 4)), dma((2, 4)),
        ],
        compiler_params=params(0),
        name="bucket_round",
    )(src, rel, dst, count, neg_rows, home, visit, visit_state, relation)


def adagrad(table, state, grad_in, axis):
    state_new = state + jnp.sum(grad_in * grad_in, axis=axis, keepdims=True) * (1.0 / grad_in.shape[axis])
    return table - LEARN_RATE * grad_in / (jnp.sqrt(state_new) + ADAGRAD_EPS), state_new


def update_kernel(
    home_grad_ref, home_ref, home_state_ref, visit_ref, visit_state_ref,
    quarter_ref, relation_ref, relation_state_ref,
    home_out, home_state_out, visit_out, visit_state_out, relation_out, relation_state_out,
):
    f32 = jnp.float32
    home_out[...], home_state_out[...] = adagrad(home_ref[...], home_state_ref[...], home_grad_ref[...], 0)
    visit_out[...] = visit_ref[...]
    visit_state_out[...] = visit_state_ref[...]
    grad = jnp.concatenate(
        [quarter_ref[c][:, first : first + QPART] for first in (0, QIM) for c in range(4)], axis=1
    )[:OWN_RELS]
    diagonal = lax.broadcasted_iota(jnp.int32, (OWN_RELS, OWN_RELS), 0) == lax.broadcasted_iota(
        jnp.int32, (OWN_RELS, OWN_RELS), 1
    )
    state = jnp.sum(jnp.where(diagonal, relation_state_ref[...], 0.0), axis=1, keepdims=True)
    relation_out[...], state = adagrad(relation_ref[...], state, grad, 1)
    relation_state_out[...] = jnp.sum(jnp.where(diagonal, state, 0.0), axis=0, keepdims=True)


def update(*arrays):
    shape = lambda a: jax.ShapeDtypeStruct(a.shape, jnp.float32)
    return pl.pallas_call(
        update_kernel,
        out_shape=tuple(shape(arrays[i]) for i in (1, 2, 3, 4, 6, 7)),
        in_specs=[VMEM] * 8,
        out_specs=(VMEM,) * 6,
        compiler_params=params(),
        name="update",
    )(*arrays)


def shards(
    home_table, home_state, visit_table, visit_state, relation_table, relation_state,
    edge_src, edge_rel, edge_dst, edge_count, neg_rows,
):
    home_grad, moved, moved_state, quarters = bucket_round(
        edge_src[0], edge_rel[0], edge_dst[0], edge_count, neg_rows,
        home_table, visit_table, visit_state[None], relation_table.T,
    )
    new_home, new_home_state, new_visit, new_visit_state, new_relation, new_relation_state = update(
        home_grad, home_table, home_state[None], moved, moved_state,
        quarters, relation_table.T, relation_state[None],
    )
    return (new_home, new_home_state[0], new_visit, new_visit_state[0], new_relation.T, new_relation_state[0])


def solution(mesh):
    cols = P(None, ("blk", "span"))
    rows = P(("blk", "span"))
    slot = P("blk", "span", None)
    return jax.shard_map(
        shards,
        mesh=mesh,
        in_specs=(cols, rows, cols, rows, cols, rows, slot, slot, slot, P("blk", "span"), P("blk", None)),
        out_specs=(cols, rows, cols, rows, cols, rows),
        check_vma=False,
    )
```

```python
import functools

import jax
import jax.numpy as jnp
from jax import lax
from jax.experimental import pallas as pl
from jax.experimental.pallas import tpu as pltpu
from jax.sharding import PartitionSpec as P

LEARN_RATE = 0.1
ADAGRAD_EPS = 1e-10
MESH = pl.DeviceIdType.MESH
LIVE = 1536
SHARE = 384
QROWS = 112
QPART = 50
QIM = 56
OWN_RELS = 29
VMEM = pl.BlockSpec(memory_space=pltpu.VMEM)
SMEM = pl.BlockSpec(memory_space=pltpu.SMEM)
NT = (((1,), (1,)), ((), ()))


def params(collective_id=None):
    if collective_id is None:
        return pltpu.CompilerParams(vmem_limit_bytes=56 * 2**20)
    return pltpu.CompilerParams(
        vmem_limit_bytes=56 * 2**20, collective_id=collective_id, has_side_effects=True
    )


def place():
    blk = lax.axis_index("blk")
    span = lax.axis_index("span")
    yh = lax.div(blk, 32)
    z = lax.rem(lax.div(blk, 4), 8)
    x = lax.rem(blk, 4)
    return yh, z, x, span


def device(yh, z, x, span):
    return (yh * 32 + lax.rem(z + 8, 8) * 4 + lax.rem(x + 4, 4), lax.rem(span, 4))


def remote(src, dst, send, recv, where):
    return pltpu.make_async_remote_copy(
        src_ref=src, dst_ref=dst, send_sem=send, recv_sem=recv, device_id=where, device_id_type=MESH
    )


def greet(peers):
    barrier = pltpu.get_barrier_semaphore()
    for peer in peers:
        pl.semaphore_signal(barrier, inc=1, device_id=peer, device_id_type=MESH)


def greeted(peers):
    pl.semaphore_wait(pltpu.get_barrier_semaphore(), len(peers))


def one_hot(rows, index):
    row = lax.broadcasted_iota(jnp.int32, (rows, index.shape[1]), 0)
    return jnp.where(row == index, 1.0, 0.0).astype(jnp.bfloat16)


def halves(value):
    high = value.astype(jnp.bfloat16)
    return high, (value - high.astype(jnp.float32)).astype(jnp.bfloat16)


def hot_lanes(low_hot, hot, group, first):
    for k in range(4):
        mask = jnp.where(group == first + k, 1.0, 0.0).astype(jnp.bfloat16)
        hot[k * 128 : (k + 1) * 128, :] = low_hot[...] * mask


FAR = {("r", 0): 4, ("r", 1): 3, ("l", 0): 3, ("l", 1): 4}


def round_kernel(
    src_ref, rel_ref, dst_ref, count_ref, neg_ref, home_ref, visit_ref, visit_state_ref, relation_ref,
    home_grad_ref, visit_out, visit_state_out, quarter_ref,
    low, low_all, piece, got_piece, index, table, low_hot, hot, total, mine, picked,
    hot_neg, negatives, rel_grad, rel_got, both, grads,
    r_buf, r_got, l_buf, l_got, row_sum, x_got, x_sum, y_got, q_buf, m_got, o_buf, o_got, moved, moved_state,
    negatives_t, kept, cast, x_in, one_buf, one_got,
    i_send, i_recv, p_send, p_recv, h_send, h_recv, y_send, y_recv, x_send, x_recv,
    r_send, r_recv, l_send, l_recv, k_send, k_recv, v_send, v_recv, a_send, a_recv,
    rr_send, rr_recv, ll_send, ll_recv, xx_send, xx_recv, yy_send, yy_recv, q_send, q_recv,
    m_send, m_recv, o_send, o_recv, b_send, b_recv, c_send, c_recv, w_send, w_recv,
    xb_send, xb_recv, e_send, e_recv,
):
    f32, bf16 = jnp.float32, jnp.bfloat16
    yh, z, x, s = place()
    yo = 1 - yh
    blk = lax.axis_index("blk")
    span_peers = [device(yh, z, x, s + d) for d in (1, 2, 3)]
    x_peers = [device(yh, z, x + d, s) for d in (1, 2, 3)]
    y_peer = device(yo, z, x, s)
    right = device(yh, z + 1, x, s)
    left = device(yh, z - 1, x, s)
    after = (lax.rem(blk + 1, 64), s)
    before = (lax.rem(blk + 63, 64), s)
    mate_span = lax.div(s, 2) * 2 + 1 - lax.rem(s, 2)
    mate = device(yh, z, x, mate_span)
    across_span = lax.rem(s + 2, 4)
    across = device(yh, z, x, across_span)
    across_mate = lax.rem(mate_span + 2, 4)
    peers = span_peers + x_peers + [y_peer, right, left, after, before]
    greet(peers)

    middle = 4 * QPART
    spare = jnp.zeros((32 - OWN_RELS, 2 * middle), f32)
    operators = jnp.concatenate([relation_ref[...], spare], axis=0)
    for c in range(4):
        re = operators[:, c * QPART : (c + 1) * QPART]
        im = operators[:, middle + c * QPART : middle + (c + 1) * QPART]
        pad = jnp.zeros((32, QIM - QPART), f32)
        rest = jnp.zeros((32, 128 - QIM - QPART), f32)
        piece[c] = jnp.concatenate([re, pad, im, rest], axis=1).astype(bf16)
    greeted(peers)
    started = []

    def go(copy):
        copy.start()
        started.append(copy)
        return copy

    def to_span(src_of, dst, send, recv):
        return [
            go(remote(src_of(lax.rem(s + d, 4)), dst, send.at[d - 1], recv.at[d - 1], span_peers[d - 1]))
            for d in (1, 2, 3)
        ]

    pieces = to_span(lambda peer: piece.at[peer], got_piece.at[s], p_send, p_recv)
    rel = rel_ref[...]
    owner = jnp.right_shift(rel * 4520, 17)
    index[s] = jnp.concatenate(
        [
            src_ref[...],
            rel + owner * (32 - OWN_RELS),
            dst_ref[...] + s * 256,
            jnp.broadcast_to(count_ref[...], (1, 1024)),
            jnp.zeros((4, 1024), jnp.int32),
        ],
        axis=0,
    )
    lists = to_span(lambda peer: index.at[s], index.at[s], i_send, i_recv)
    got_piece[s] = piece[s]
    for copy in pieces:
        copy.wait_recv()
    block = jnp.concatenate([got_piece[c].astype(f32) for c in range(4)], axis=0).T
    table[yh, z, x] = block[:QROWS].astype(bf16)

    own = table.at[yh, z, x]
    other = table.at[yo, z, x]
    y_copy = go(remote(own, own, y_send, y_recv, y_peer))
    x_copies = [
        go(remote(own, own, x_send.at[d - 1], x_recv.at[d - 1], x_peers[d - 1])) for d in (1, 2, 3)
    ]
    low[0] = home_ref[...].astype(bf16)
    low[1] = visit_ref[...].astype(bf16)
    low_all[s] = low[...]
    lows = [[], []]
    for k in (0, 1):
        for number, peer in enumerate((across, mate)):
            lows[k].append(
                go(remote(low.at[k], low_all.at[s, k], h_send.at[k, number], h_recv.at[k, number], peer))
            )

    def relay(k):
        lows[k][0].wait_recv()
        ref = low_all.at[across_span, k]
        lows[k].append(go(remote(ref, ref, h_send.at[k, 2], h_recv.at[k, 2], mate)))

    for copy in lists:
        copy.wait_recv()

    at = lax.broadcasted_iota(jnp.int32, (8, LIVE), 1)
    kind = lax.broadcasted_iota(jnp.int32, (8, LIVE), 0)
    slots = jnp.full((8, LIVE), -1, jnp.int32)
    start = jnp.zeros((1, 1), jnp.int32)
    for c in range(4):
        part = index[c]
        end = start + part[3:4, 0:1]
        listed = jnp.concatenate([part, jnp.zeros((8, LIVE - 1024), jnp.int32)], axis=1)
        if c:
            for bit in range(11):
                on = jnp.bitwise_and(jnp.right_shift(start, bit), 1) == 1
                listed = jnp.where(on, pltpu.roll(listed, 1 << bit, 1), listed)
        slots = jnp.where((at >= start) & (at < end), listed, slots)
        start = end
    slots = jnp.where(kind == 3, jnp.where(at < start, 1, 0), slots)
    share_slots = jnp.zeros((8, SHARE), jnp.int32)
    for c in range(4):
        share_slots = jnp.where(s == c, slots[:, c * SHARE : (c + 1) * SHARE], share_slots)
    spot = slots[1:2]
    group = jnp.right_shift(spot, 7)
    low_hot[...] = one_hot(128, jnp.bitwise_and(spot, 127))
    total[...] = jnp.zeros_like(total)

    def half(chunk):
        return yh if chunk == 0 else yo

    def gather(chunk, zz):
        zz = lax.rem(zz + 8, 8)
        hot_lanes(low_hot, hot, group, half(chunk) * 32 + zz * 4)
        block = jnp.concatenate([table[half(chunk), zz, k] for k in range(4)], axis=1)
        total[...] += jnp.dot(block, hot[...], preferred_element_type=f32)

    flying = {}
    turns = {"r": 3, "l": 4}
    rows = {}

    def pass_on(way, step, key, send, recv, ref):
        flying[(key, way, step)] = go(remote(ref, ref, send, recv, right if way == "r" else left))

    def along_x(number, ref):
        rows[number] = [
            go(remote(ref, ref, w_send.at[number, d - 1], w_recv.at[number, d - 1], x_peers[d - 1]))
            for d in (1, 2, 3)
        ]

    def gather_row(number, zz):
        for copy in rows[number]:
            copy.wait_recv()
        gather(1, zz)

    for step in range(5):
        if step == 0:
            y_copy.wait_recv()
            along_x(0, other)
        for way in ("r", "l"):
            zz = z - step if way == "r" else z + step
            ref = table.at[yo, lax.rem(zz + 8, 8), x]
            if 1 <= step <= turns[way]:
                flying[("other", way, step - 1)].wait_recv()
            if step < turns[way]:
                send, recv = (b_send, b_recv) if way == "r" else (c_send, c_recv)
                pass_on(way, step, "other", send.at[step], recv.at[step], ref)
            if 1 <= step <= turns[way]:
                along_x(step if way == "r" else 3 + step, ref)
        if step == 0:
            for copy in x_copies:
                copy.wait_recv()
        for part in (0, 1):
            for way in ("r", "l"):
                if 1 <= step <= FAR[(way, part)]:
                    flying[(part, way, step - 1)].wait_recv()
                if step < FAR[(way, part)]:
                    zz = z - step if way == "r" else z + step
                    ref = table.at[yh, lax.rem(zz + 8, 8), pl.ds(2 * part, 2)]
                    send, recv = (r_send, r_recv) if way == "r" else (l_send, l_recv)
                    pass_on(way, step, part, send.at[part, step], recv.at[part, step], ref)
        if step == 0:
            gather(0, z)
        else:
            gather(0, z - step)
            if step < 4:
                gather(0, z + step)
            if step == 1:
                gather_row(0, z)
            else:
                gather_row(step - 1, z - step + 1)
                gather_row(step + 2, z + step - 1)
        if step in (1, 2):
            relay(step - 1)
    gather_row(7, z + 4)
    for c in range(4):
        mine[c] = total[:, c * SHARE : (c + 1) * SHARE].astype(bf16)
    picks = to_span(lambda peer: mine.at[peer], picked.at[s], k_send, k_recv)
    picked[s] = mine[s]

    for copy in lows[0][1:]:
        copy.wait_recv()
    hot_neg[...] = one_hot(1024, neg_ref[...])
    home = jnp.concatenate([low_all[c, 0] for c in range(4)], axis=1)
    found = jnp.dot(home, hot_neg[...], preferred_element_type=f32)
    negatives[...] = found.astype(bf16)
    negatives_t[...] = found.T.astype(bf16)
    for copy in lows[1][1:]:
        copy.wait_recv()
    visit = jnp.concatenate([low_all[c, 1] for c in range(4)], axis=1)
    live = share_slots[3:4, :].astype(f32)
    hot_source = one_hot(1024, share_slots[0:1, :])
    hot_dest = one_hot(1024, share_slots[2:3, :])
    source = jnp.dot(home, hot_source, preferred_element_type=f32)
    dest = jnp.dot(visit, hot_dest, preferred_element_type=f32)
    dest_re, dest_im = dest[:middle], dest[middle:]
    for copy in picks:
        copy.wait_recv()
    rel = [picked[c].astype(f32) for c in range(4)]
    rel_re = jnp.concatenate([part[:QPART] for part in rel], axis=0)
    rel_im = jnp.concatenate([part[QIM : QIM + QPART] for part in rel], axis=0)
    trans = jnp.concatenate(
        [rel_re * dest_re - rel_im * dest_im, rel_re * dest_im + rel_im * dest_re], axis=0
    ).astype(bf16)
    positive = jnp.sum(source * trans.astype(f32), axis=0, keepdims=True)
    score = jnp.dot(negatives_t[...], trans, preferred_element_type=f32)
    pos_weight = -live * jax.nn.sigmoid(-positive)
    weight = (live * jax.nn.sigmoid(score) * (1.0 / 1024.0)).astype(bf16)
    pull = jnp.dot(negatives[...], weight, preferred_element_type=f32)
    grad = pos_weight * source + pull
    grad_re, grad_im = grad[:middle], grad[middle:]
    out_re = dest_re * grad_re + dest_im * grad_im
    out_im = dest_re * grad_im - dest_im * grad_re
    pad = jnp.zeros((QIM - QPART, SHARE), f32)
    for c in range(4):
        part = slice(c * QPART, (c + 1) * QPART)
        high, rest = halves(jnp.concatenate([out_re[part], pad, out_im[part], pad], axis=0))
        rel_grad[0, c] = high
        rel_grad[1, c] = rest
    swaps = [
        to_span(lambda peer: rel_grad.at[i, peer], rel_got.at[i, s], a_send.at[i], a_recv.at[i]) for i in (0, 1)
    ]
    for i in (0, 1):
        rel_got[i, s] = rel_grad[i, s]
    grad_dest = jnp.concatenate(
        [rel_re * grad_re + rel_im * grad_im, rel_re * grad_im - rel_im * grad_re], axis=0
    )
    dest_high, dest_low = halves(grad_dest)
    visit_grad = lax.dot_general(dest_high, hot_dest, NT, preferred_element_type=f32) + lax.dot_general(
        dest_low, hot_dest, NT, preferred_element_type=f32
    )
    m_copies = {}

    def to_mate(k):
        for i, row in ((1, across_mate), (0, mate_span)):
            m_copies[(i, k)] = go(remote(grads.at[row, k], m_got.at[i, k], m_send.at[i, k], m_recv.at[i, k], mate))

    for c in range(4):
        grads[c, 1] = visit_grad[:, c * 256 : (c + 1) * 256]
    to_mate(1)
    share = jnp.dot(hot_neg[...], weight, preferred_element_type=f32) + pos_weight * hot_source.astype(f32)
    share_high, share_low = halves(share)
    home_grad = lax.dot_general(trans, share_high, NT, preferred_element_type=f32) + lax.dot_general(
        trans, share_low, NT, preferred_element_type=f32
    )
    for c in range(4):
        grads[c, 0] = home_grad[:, c * 256 : (c + 1) * 256]
    to_mate(0)

    def take(i):
        for copy in swaps[i]:
            copy.wait_recv()
        for c in range(4):
            both[i * QROWS : (i + 1) * QROWS, c * SHARE : (c + 1) * SHARE] = rel_got[i, c]

    def scatter(chunk, zz, fine=True):
        hot_lanes(low_hot, hot, group, half(chunk) * 32 + lax.rem(zz + 8, 8) * 4)
        if fine:
            sums = lax.dot_general(both[...], hot[...], NT, preferred_element_type=f32)
            sums = sums[:QROWS] + sums[QROWS:]
        else:
            sums = lax.dot_general(both[:QROWS], hot[...], NT, preferred_element_type=f32)
        return [sums[:, k * 128 : (k + 1) * 128] for k in range(4)]

    back = {}

    def ring(dist):
        value = None
        for way in ("r", "l"):
            zz = z + dist if way == "r" else z - dist
            buf, got, send, recv = (
                (r_buf, r_got, rr_send, rr_recv) if way == "r" else (l_buf, l_got, ll_send, ll_recv)
            )
            if dist < 4 or value is None:
                value = scatter(0, zz, dist < 3)
            for part in (0, 1):
                if dist > FAR[(way, part)]:
                    continue
                if dist < FAR[(way, part)]:
                    back[(part, way, dist + 1)].wait_recv()
                for k in (0, 1):
                    here = value[2 * part + k]
                    if dist < FAR[(way, part)]:
                        here = here + got[part, dist, k].astype(f32)
                    buf[part, dist - 1, k] = here.astype(bf16)
                back[(part, way, dist)] = go(
                    remote(
                        buf.at[part, dist - 1], got.at[part, dist - 1],
                        send.at[part, dist - 1], recv.at[part, dist - 1],
                        right if way == "r" else left,
                    )
                )

    x_rows = {}

    def sow(number, zz, fine=True):
        value = scatter(1, zz, fine)
        for k in range(4):
            kept[number, k] = value[k]
            cast[number, k] = value[k].astype(bf16)
        x_rows[number] = [
            go(
                remote(
                    cast.at[number, lax.rem(x + d, 4)], x_in.at[number, d - 1],
                    xb_send.at[number, d - 1], xb_recv.at[number, d - 1], x_peers[d - 1],
                )
            )
            for d in (1, 2, 3)
        ]

    def reap(number):
        for copy in x_rows[number]:
            copy.wait_recv()
        return kept[number, x] + sum(x_in[number, d].astype(f32) for d in range(3))

    def ring_row(dist):
        for i, way in enumerate(("r", "l")):
            if dist > turns[way]:
                continue
            value = reap(dist if way == "r" else 3 + dist)
            if dist < turns[way]:
                back[("other", way, dist + 1)].wait_recv()
                value = value + one_got[i, dist]
            one_buf[i, dist - 1] = value
            back[("other", way, dist)] = go(
                remote(
                    one_buf.at[i, dist - 1], one_got.at[i, dist - 1],
                    e_send.at[i, dist - 1], e_recv.at[i, dist - 1], right if way == "r" else left,
                )
            )

    o_copies = {}

    def cross(k):
        m_copies[(1, k)].wait_recv()
        o_buf[k] = (grads[across_span, k] + m_got[1, k]).astype(bf16)
        o_copies[k] = go(remote(o_buf.at[k], o_got.at[k], o_send.at[k], o_recv.at[k], across))

    def summed(k):
        m_copies[(0, k)].wait_recv()
        o_copies[k].wait_recv()
        return grads[s, k] + m_got[0, k] + o_got[k].astype(f32)

    take(0)
    ring(4)
    sow(7, z - 4, False)
    cross(1)
    sow(3, z + 3, False)
    sow(6, z - 3, False)
    ring(3)
    ring_row(4)
    take(1)
    cross(0)
    sow(2, z + 2)
    sow(5, z - 2)
    ring(2)
    ring_row(3)
    sow(1, z + 1)
    sow(4, z - 1)
    ring(1)
    ring_row(2)
    moved[...], moved_state[...] = adagrad(visit_ref[...], visit_state_ref[...], summed(1), 0)
    sow(0, z)
    ring_row(1)
    near = scatter(0, z)
    for part in (0, 1):
        back[(part, "r", 1)].wait_recv()
        back[(part, "l", 1)].wait_recv()
        for k in (0, 1):
            row_sum[2 * part + k] = (
                near[2 * part + k] + r_got[part, 0, k].astype(f32) + l_got[part, 0, k].astype(f32)
            )
    x_copies = [
        go(
            remote(
                row_sum.at[lax.rem(x + d, 4)], x_got.at[d - 1],
                xx_send.at[d - 1], xx_recv.at[d - 1], x_peers[d - 1],
            )
        )
        for d in (1, 2, 3)
    ]
    moves = [
        go(remote(moved, visit_out, v_send.at[0], v_recv.at[0], after)),
        go(remote(moved_state, visit_state_out, v_send.at[1], v_recv.at[1], after)),
    ]
    for way in ("r", "l"):
        back[("other", way, 1)].wait_recv()
    x_sum[...] = reap(0) + one_got[0, 0] + one_got[1, 0]
    y_copy = go(remote(x_sum, y_got, yy_send, yy_recv, y_peer))
    home_grad_ref[...] = summed(0)
    for copy in x_copies:
        copy.wait_recv()
    here = row_sum[x] + x_got[0] + x_got[1] + x_got[2]
    y_copy.wait_recv()
    turned = jnp.concatenate([here + y_got[...], jnp.zeros((128 - QROWS, 128), f32)], axis=0).T
    for c in range(4):
        q_buf[c] = turned[32 * c : 32 * (c + 1)]
    quarter_ref[s] = q_buf[s]
    for copy in to_span(lambda peer: q_buf.at[peer], quarter_ref.at[s], q_send, q_recv) + moves:
        copy.wait_recv()
    for copy in started:
        copy.wait_send()


def bucket_round(src, rel, dst, count, neg_rows, home, visit, visit_state, relation):
    dma = pltpu.SemaphoreType.DMA
    bf16, f32, i32 = jnp.bfloat16, jnp.float32, jnp.int32
    pair = (2,) + home.shape
    quarters = (4, QROWS, SHARE)
    ring = pltpu.VMEM((2, 4, 2, QROWS, 128), bf16)
    lone = pltpu.VMEM((2, 4, QROWS, 128), f32)
    rows = home.shape[0]
    return pl.pallas_call(
        round_kernel,
        out_shape=(
            jax.ShapeDtypeStruct(home.shape, f32),
            jax.ShapeDtypeStruct(visit.shape, f32),
            jax.ShapeDtypeStruct(visit_state.shape, f32),
            jax.ShapeDtypeStruct((4, 32, 128), f32),
        ),
        in_specs=[VMEM] * 9,
        out_specs=(VMEM,) * 4,
        scratch_shapes=[
            pltpu.VMEM(pair, bf16), pltpu.VMEM((4,) + pair, bf16),
            pltpu.VMEM((4, 32, 128), bf16), pltpu.VMEM((4, 32, 128), bf16),
            pltpu.VMEM((4, 8, 1024), i32), pltpu.VMEM((2, 8, 4, QROWS, 128), bf16),
            pltpu.VMEM((128, LIVE), bf16), pltpu.VMEM((512, LIVE), bf16), pltpu.VMEM((QROWS, LIVE), f32),
            pltpu.VMEM(quarters, bf16), pltpu.VMEM(quarters, bf16),
            pltpu.VMEM((1024, 1024), bf16), pltpu.VMEM((rows, 1024), bf16),
            pltpu.VMEM((2,) + quarters, bf16), pltpu.VMEM((2,) + quarters, bf16), pltpu.VMEM((2 * QROWS, LIVE), bf16),
            pltpu.VMEM((4,) + pair, f32),
            ring, ring, ring, ring,
            pltpu.VMEM((4, QROWS, 128), f32), pltpu.VMEM((3, QROWS, 128), f32),
            pltpu.VMEM((QROWS, 128), f32), pltpu.VMEM((QROWS, 128), f32), pltpu.VMEM((4, 32, 128), f32),
            pltpu.VMEM((2,) + pair, f32), pltpu.VMEM(pair, bf16), pltpu.VMEM(pair, bf16),
            pltpu.VMEM(visit.shape, f32), pltpu.VMEM(visit_state.shape, f32),
            pltpu.VMEM((1024, rows), bf16), pltpu.VMEM((8, 4, QROWS, 128), f32), pltpu.VMEM((8, 4, QROWS, 128), bf16),
            pltpu.VMEM((8, 3, QROWS, 128), bf16), lone, lone,
            dma((3,)), dma((3,)), dma((3,)), dma((3,)), dma((2, 3)), dma((2, 3)), dma, dma,
            dma((3,)), dma((3,)), dma((2, 4)), dma((2, 4)), dma((2, 4)), dma((2, 4)),
            dma((3,)), dma((3,)), dma((3,)), dma((3,)), dma((2, 3)), dma((2, 3)),
            dma((2, 4)), dma((2, 4)), dma((2, 4)), dma((2, 4)), dma((3,)), dma((3,)),
            dma, dma, dma((3,)), dma((3,)), dma((2, 2)), dma((2, 2)), dma((2,)), dma((2,)),
            dma((4,)), dma((4,)), dma((4,)), dma((4,)), dma((8, 3)), dma((8, 3)),
            dma((8, 3)), dma((8, 3)), dma((2, 4)), dma((2, 4)),
        ],
        compiler_params=params(0),
        name="bucket_round",
    )(src, rel, dst, count, neg_rows, home, visit, visit_state, relation)


def adagrad(table, state, grad_in, axis):
    state_new = state + jnp.sum(grad_in * grad_in, axis=axis, keepdims=True) * (1.0 / grad_in.shape[axis])
    return table - LEARN_RATE * grad_in / (jnp.sqrt(state_new) + ADAGRAD_EPS), state_new


def update_kernel(
    home_grad_ref, home_ref, home_state_ref, visit_ref, visit_state_ref,
    quarter_ref, relation_ref, relation_state_ref,
    home_out, home_state_out, visit_out, visit_state_out, relation_out, relation_state_out,
):
    f32 = jnp.float32
    home_out[...], home_state_out[...] = adagrad(home_ref[...], home_state_ref[...], home_grad_ref[...], 0)
    visit_out[...] = visit_ref[...]
    visit_state_out[...] = visit_state_ref[...]
    grad = jnp.concatenate(
        [quarter_ref[c][:, first : first + QPART] for first in (0, QIM) for c in range(4)], axis=1
    )[:OWN_RELS]
    diagonal = lax.broadcasted_iota(jnp.int32, (OWN_RELS, OWN_RELS), 0) == lax.broadcasted_iota(
        jnp.int32, (OWN_RELS, OWN_RELS), 1
    )
    state = jnp.sum(jnp.where(diagonal, relation_state_ref[...], 0.0), axis=1, keepdims=True)
    relation_out[...], state = adagrad(relation_ref[...], state, grad, 1)
    relation_state_out[...] = jnp.sum(jnp.where(diagonal, state, 0.0), axis=0, keepdims=True)


def update(*arrays):
    shape = lambda a: jax.ShapeDtypeStruct(a.shape, jnp.float32)
    return pl.pallas_call(
        update_kernel,
        out_shape=tuple(shape(arrays[i]) for i in (1, 2, 3, 4, 6, 7)),
        in_specs=[VMEM] * 8,
        out_specs=(VMEM,) * 6,
        compiler_params=params(),
        name="update",
    )(*arrays)


def shards(
    home_table, home_state, visit_table, visit_state, relation_table, relation_state,
    edge_src, edge_rel, edge_dst, edge_count, neg_rows,
):
    home_grad, moved, moved_state, quarters = bucket_round(
        edge_src[0], edge_rel[0], edge_dst[0], edge_count, neg_rows,
        home_table, visit_table, visit_state[None], relation_table.T,
    )
    new_home, new_home_state, new_visit, new_visit_state, new_relation, new_relation_state = update(
        home_grad, home_table, home_state[None], moved, moved_state,
        quarters, relation_table.T, relation_state[None],
    )
    return (new_home, new_home_state[0], new_visit, new_visit_state[0], new_relation.T, new_relation_state[0])


def solution(mesh):
    cols = P(None, ("blk", "span"))
    rows = P(("blk", "span"))
    slot = P("blk", "span", None)
    return jax.shard_map(
        shards,
        mesh=mesh,
        in_specs=(cols, rows, cols, rows, cols, rows, slot, slot, slot, P("blk", "span"), P("blk", None)),
        out_specs=(cols, rows, cols, rows, cols, rows),
        check_vma=False,
    )
```
